512 devices in a mesh: seq: 16 (over x, z_lo), head: 8 (over z_hi, core), pool: 4 (over y).
Axes of the slice: x: 4, y: 4, z: 16 (z_hi: 4, z_lo: 4; z = z_hi * 4 + z_lo), core: 2. Of those that a mesh axis runs over, the one named last changes fastest.
Arguments:
- mixer_input: bfloat16 [4, 3072, 16384], P('pool', 'seq', 'head'), may hold values from -6 to 6
- gate_input: bfloat16 [4, 3072, 16384], P('pool', 'seq', 'head'), may hold values from -16 to 16
- input_coeff: bfloat16 [4, 3072, 2048], P('pool', 'seq', 'head'), may hold values from -0.375 to 0.375
- output_coeff: bfloat16 [4, 3072, 2048], P('pool', 'seq', 'head'), may hold values from -0.109375 to 0.109375
- log_decay: float32 [4, 256, 3072], P('pool', 'head', 'seq'), may hold values from -2 to 0
- skip_gain: float32 [256], P('head'), may hold values from 0.1 to 1.9
- norm_gain: float32 [16384], P('head'), may hold values from 0.1 to 1.9
- segment_ids: int32 [4, 3072], P('pool', 'seq'), may hold values from 0 to 2, never falling along the last dimension, each value on 1 to 2304 neighbouring positions
- query_rows: bfloat16 [4, 3072, 8192], P('pool', 'seq', 'head'), may hold values from -5 to 5
- key_rows: bfloat16 [4, 3072, 1024], P('pool', 'seq', 'head'), may hold values from -5 to 5
- value_rows: bfloat16 [4, 3072, 1024], P('pool', 'seq', 'head'), may hold values from -6 to 6
- owner_map: int32 [4, 32], P('pool', 'head'), may hold values from 0 to 3, as said below
Outputs:
- mixer_output: bfloat16 [4, 3072, 16384], P('pool', 'seq', 'head')
- attention_out: bfloat16 [4, 3072, 8192], P('pool', 'seq', 'head')
- owned_states: float32 [4, 4, 64, 64, 256], P('pool', None, 'head', 'seq')
- owned_keys: bfloat16 [4, 4, 768, 1024], P('pool', None, 'seq', 'head')
- owned_values: bfloat16 [4, 4, 768, 1024], P('pool', None, 'seq', 'head')
The draws below stay inside these ranges and needn't reach their ends.
Inputs may be any that keep to these rules, and one draw needn't show every extreme that they name: `owner_map`: for each request and each run of 4 consecutive hand-over groups starting at a multiple of 4, the owners are 0 to 3, each once.
All inputs are finite; a program needn't handle non-finite values.
Results may differ from the reference program's by a relative error of at most 0.0055.
Values may be sent and summed in bfloat16 or wider, within the bound.
A program may use at most 128 MiB of HBM per device.

```python
import math
import jax
import jax.numpy as jnp
import numpy as np
from jax import lax

HEADS = 256
HEAD_P = 64
STATE = 256
SSM_GROUPS = 8
QHEADS = 64
KV_HEADS = 8
HEAD_DIM = 128
TOK_DEV = 192
SEGS = 3
WINDOW_LENGTH = 3072
REQUEST_COUNT = 4
HGROUPS = 32
N_SEQ = 16
N_HEAD = 8
N_POOL = 4


def paired_rows(key, strength):
    key_query, key_keys, key_sign = jax.random.split(key, 3)
    query = jnp.clip(jax.random.normal(key_query, (REQUEST_COUNT, WINDOW_LENGTH, QHEADS * HEAD_DIM), jnp.float32), -5.0, 5.0)
    keys_drawn = jnp.clip(jax.random.normal(key_keys, (REQUEST_COUNT, WINDOW_LENGTH, KV_HEADS * HEAD_DIM), jnp.float32), -5.0, 5.0)
    positions = jnp.arange(WINDOW_LENGTH)
    chosen = (positions % 97 == 50) & (strength > 0.5)
    amplitude = 3.0 + (positions // 97 % 3).astype(jnp.float32)
    signs = jnp.where(jax.random.bernoulli(key_sign, 0.5, (REQUEST_COUNT, WINDOW_LENGTH, KV_HEADS, HEAD_DIM)), 1.0, -1.0)
    aligned = signs * amplitude[None, :, None, None]
    q_aligned = jnp.repeat(aligned, QHEADS // KV_HEADS, axis=2).reshape(REQUEST_COUNT, WINDOW_LENGTH, QHEADS * HEAD_DIM)
    query = jnp.where(chosen[None, :, None], q_aligned, query)
    keys_drawn = jnp.where(chosen[None, :, None], aligned.reshape(REQUEST_COUNT, WINDOW_LENGTH, KV_HEADS * HEAD_DIM), keys_drawn)
    lowered_value = amplitude - 2.0 * HEAD_DIM ** 0.5 / amplitude
    lowered = aligned.at[..., 0].set(signs[..., 0] * lowered_value[None, :, None])
    shifted = jnp.roll(lowered.reshape(REQUEST_COUNT, WINDOW_LENGTH, KV_HEADS * HEAD_DIM), -1, axis=1)
    earlier_row = jnp.roll(chosen, -1)
    keys_drawn = jnp.where(earlier_row[None, :, None], shifted, keys_drawn)
    return (query, keys_drawn)


def draw_query_rows(key, part):
    strength = 0.0
    query, keys_drawn = paired_rows(key, strength)
    return query.astype(jnp.bfloat16)


def draw_key_rows(key, part):
    strength = 0.0
    query, keys_drawn = paired_rows(key, strength)
    return keys_drawn.astype(jnp.bfloat16)


def decay_law(key, low_rate, high_rate):
    speed_random_key, coarse_random_key, spike_random_key, nesting_random_key = jax.random.split(key, 4)
    speed_level = jnp.exp(jax.random.uniform(speed_random_key, (REQUEST_COUNT, HEADS, 1), jnp.float32, math.log(low_rate), math.log(high_rate))) / WINDOW_LENGTH
    coarse_value = jax.random.uniform(coarse_random_key, (REQUEST_COUNT, HEADS, WINDOW_LENGTH), jnp.float32, 0.5, 2.0)
    spike_amount = jax.random.randint(spike_random_key, (REQUEST_COUNT, 1, WINDOW_LENGTH), 0, WINDOW_LENGTH) < 2
    nesting_level = jax.random.uniform(nesting_random_key, (REQUEST_COUNT, HEADS, WINDOW_LENGTH), jnp.float32, math.log(0.5), math.log(0.8))
    steady_level = jnp.maximum(-speed_level * coarse_value, -2.0)
    return jnp.where(spike_amount, nesting_level, steady_level)


def draw_log_decay(key, part):
    key = jax.random.fold_in(key, 11)
    return decay_law(key, 0.01, 100.0)


def gate_law(base, spread):
    head_pos = (jnp.arange(HEADS * HEAD_P) // HEAD_P).astype(jnp.float32) / max(HEADS - 1, 1)
    return (base * jnp.exp(spread * head_pos)[None, None, :]).astype(jnp.bfloat16)


def draw_gate_input(key, part):
    key = jax.random.fold_in(key, 3)
    base = jnp.clip(jax.random.normal(key, (REQUEST_COUNT, WINDOW_LENGTH, HEADS * HEAD_P), jnp.float32), -4.0, 4.0)
    return gate_law(base, math.log(3.0))


def draw_owner_map(key, part):
    key = jax.random.fold_in(key, 7)
    scores = jax.random.randint(key, (REQUEST_COUNT, HGROUPS // REQUEST_COUNT, REQUEST_COUNT), 0, 1 << 20) * REQUEST_COUNT + jnp.arange(REQUEST_COUNT)[None, None, :]
    order = jnp.argsort(scores, axis=-1, stable=True).astype(jnp.int32)
    return order.reshape(REQUEST_COUNT, HGROUPS)


def steps_of(stream_key, dims, cuts, least, top_value):
    def one(axis_at, blocks):
        steps = jax.random.uniform(jax.random.fold_in(jax.random.fold_in(stream_key, 6), axis_at), (blocks,), jnp.float32, least / len(cuts), top_value / len(cuts))
        return jnp.repeat(jnp.exp(steps), dims[axis_at] // blocks).reshape((-1,) + (1,) * (len(dims) - axis_at - 1))

    level = one(*cuts[0])
    for cut in cuts[1:]:
        level = level * one(*cut)
    return level


def split_up(count, total, limit, skew):
    portions = [(1 << 20) // math.isqrt(grade ** skew) + 1 for grade in range(2, count + 1)]
    spare, given = total - limit - (count - 1), [1] * (count - 1)
    while spare > 0:
        free = [i for i in range(count - 1) if given[i] < limit]
        whole, budget = sum([portions[i] for i in free]), spare
        for i in free:
            addition = min(limit - given[i], max(1, budget * portions[i] // whole), spare)
            given[i] = given[i] + addition
            spare = spare - addition
    return np.array([limit] + given)


def ragged(key, number_of, total, bound, skew):
    if number_of == 2:
        one = jax.random.randint(key, (), max(1, total - bound), min(bound, total - 1) + 1)
        return jnp.stack([one, total - one])
    lengths = jnp.asarray(split_up(number_of, total, bound, skew), jnp.int32)
    twos = (number_of - 1) // 2
    donor, sink = lengths[1:1 + 2 * twos:2], lengths[2:2 + 2 * twos:2]
    margin = jnp.minimum(donor - 1, bound - sink)
    passed = jax.random.randint(jax.random.fold_in(key, 1), (twos,), 0, 1 << 20) % (margin + 1)
    lengths = lengths.at[1:1 + 2 * twos:2].set(donor - passed).at[2:2 + 2 * twos:2].set(sink + passed)
    return lengths[jax.random.permutation(jax.random.fold_in(key, 2), number_of)]


def scatter_about(rng, shape, scale, reach, shards=(), dtype=jnp.bfloat16):
    factor_of = steps_of(rng, shape, shards, -0.22, 0.18) if shards else 1.0
    values = jax.random.normal(rng, shape, jnp.float32) * scale * factor_of
    return jnp.minimum(jnp.maximum(values, -reach), reach).astype(dtype)


def setup_inputs(seed: int = 0) -> dict:
    keys = jax.random.split(jax.random.key(seed), 13)
    return {
        "mixer_input": scatter_about(keys[0], (REQUEST_COUNT, WINDOW_LENGTH, HEADS * HEAD_P), 1.0, 6.0, ((0, 4), (1, 16), (2, 8))),
        "gate_input": draw_gate_input(jax.random.fold_in(keys[12], 71), 0),
        "input_coeff": scatter_about(keys[2], (REQUEST_COUNT, WINDOW_LENGTH, SSM_GROUPS * STATE), STATE ** -0.5, 0.375, ((0, 4), (1, 16), (2, 8))),
        "output_coeff": scatter_about(keys[3], (REQUEST_COUNT, WINDOW_LENGTH, SSM_GROUPS * STATE), WINDOW_LENGTH ** -0.5, 0.109375, ((0, 4), (1, 16), (2, 8))),
        "log_decay": draw_log_decay(jax.random.fold_in(keys[12], 71), 0),
        "skip_gain": jnp.clip(1.0 + 0.18 * jax.random.normal(keys[5], (HEADS,), jnp.float32), 0.1, 1.9),
        "norm_gain": jnp.clip(1.0 + 0.18 * jax.random.normal(keys[6], (HEADS * HEAD_P,), jnp.float32), 0.1, 1.9),
        "segment_ids": jax.vmap(lambda own: jnp.searchsorted(jnp.cumsum(ragged(own, SEGS, WINDOW_LENGTH, WINDOW_LENGTH * 3 // 4, 0)), jnp.arange(WINDOW_LENGTH), side="right"))(jax.random.split(keys[7], REQUEST_COUNT)).reshape((REQUEST_COUNT, WINDOW_LENGTH)).astype(jnp.int32),
        "query_rows": draw_query_rows(jax.random.fold_in(keys[12], 71), 0),
        "key_rows": draw_key_rows(jax.random.fold_in(keys[12], 71), 0),
        "value_rows": scatter_about(keys[10], (REQUEST_COUNT, WINDOW_LENGTH, KV_HEADS * HEAD_DIM), 1.0, 6.0, ((0, 4), (1, 16), (2, 8))),
        "owner_map": draw_owner_map(jax.random.fold_in(keys[12], 71), 0),
    }


NORM_EPS = 1e-05
HIGH = lax.Precision.HIGHEST
MASK_LOW = -1e+30

def ssd_request(x_req, b_req, c_req, decay_req, seg_req, skip_gain):
    row_count = TOK_DEV
    per_group = HEADS // SSM_GROUPS
    x_tracts = x_req.reshape(N_SEQ, row_count, SSM_GROUPS, per_group, HEAD_P)
    b_tracts = b_req.reshape(N_SEQ, row_count, SSM_GROUPS, STATE)
    c_tracts = c_req.reshape(N_SEQ, row_count, SSM_GROUPS, STATE)
    d_tracts = decay_req.reshape(HEADS, N_SEQ, row_count).transpose(1, 0, 2)
    s_tracts = seg_req.reshape(N_SEQ, row_count)
    skip_grid = skip_gain.reshape(SSM_GROUPS, per_group)
    places = jnp.arange(row_count)

    def tract_step(carry, block):
        state_sum, prev_seg = carry
        x_blk, b_blk, c_blk, d_blk, s_blk = block
        cum = jnp.cumsum(d_blk, axis=1)
        same_seg = (s_blk[:, None] == s_blk[None, :]) & (places[:, None] >= places[None, :])
        log_gap = cum[:, :, None] - cum[:, None, :]
        decay_mask = jnp.where(same_seg[None], jnp.exp(jnp.where(same_seg[None], log_gap, 0.0)), 0.0)
        inner_prod = jnp.einsum('ign,jgn->gij', c_blk.astype(jnp.float32), b_blk.astype(jnp.float32), precision=HIGH)
        mix_weight = (inner_prod[:, None] * decay_mask.reshape(SSM_GROUPS, per_group, row_count, row_count)).astype(jnp.bfloat16)
        x_wide = x_blk.astype(jnp.float32)
        intra_part = jnp.einsum('gkij,jgkp->igkp', lax.optimization_barrier(mix_weight).astype(jnp.float32), x_wide, precision=HIGH)
        seg_float = s_blk.astype(jnp.float32)
        enter_weight = jnp.where(seg_float[None, :] == prev_seg, jnp.exp(cum), 0.0)
        carried = jnp.einsum('ign,gkpn->igkp', c_blk.astype(jnp.float32), state_sum.reshape(SSM_GROUPS, per_group, HEAD_P, STATE), precision=HIGH)
        mixed = intra_part + carried * enter_weight.T.reshape(row_count, SSM_GROUPS, per_group, 1) + skip_grid[None, :, :, None] * x_wide
        tail_weight = jnp.where((s_blk == s_blk[-1])[None, :], jnp.exp(cum[:, -1:] - cum), 0.0)
        tail_x = (x_wide * tail_weight.T.reshape(row_count, SSM_GROUPS, per_group, 1)).astype(jnp.bfloat16)
        own_state = jnp.einsum('jgkp,jgn->gkpn', lax.optimization_barrier(tail_x).astype(jnp.float32), b_blk.astype(jnp.float32), precision=HIGH)
        own_state = own_state.reshape(HEADS, HEAD_P, STATE)
        through = jnp.exp(cum[:, -1]) * jnp.where(seg_float[-1] == prev_seg, 1.0, 0.0)
        new_state = through[:, None, None] * state_sum + own_state
        return ((new_state, seg_float[-1]), mixed.astype(jnp.bfloat16).reshape(row_count, HEADS * HEAD_P))
    start_carry = (jnp.zeros((HEADS, HEAD_P, STATE), jnp.float32), jnp.array(-1.0, jnp.float32))
    (final_state, last_seg), outputs = lax.scan(tract_step, start_carry, (x_tracts, b_tracts, c_tracts, d_tracts, s_tracts))
    return (outputs.reshape(WINDOW_LENGTH, HEADS * HEAD_P), final_state)

def attend_request(q_req, k_req, v_req, seg_req):
    q_groups = QHEADS // KV_HEADS
    score_scale = HEAD_DIM ** (-0.5)
    key_all = k_req.reshape(WINDOW_LENGTH, KV_HEADS, HEAD_DIM).astype(jnp.float32)
    value_all = v_req.reshape(WINDOW_LENGTH, KV_HEADS, HEAD_DIM).astype(jnp.float32)
    key_pos = jnp.arange(WINDOW_LENGTH)
    q_blocks = q_req.reshape(N_SEQ, TOK_DEV, KV_HEADS, q_groups, HEAD_DIM)
    s_blocks = seg_req.reshape(N_SEQ, TOK_DEV)
    starts = jnp.arange(N_SEQ) * TOK_DEV

    def one_block(args):
        q_blk, s_blk, offset = args
        scores = jnp.einsum('ikqd,jkd->kqij', q_blk.astype(jnp.float32), key_all, precision=HIGH) * score_scale
        query_pos = offset + jnp.arange(TOK_DEV)
        seen = (key_pos[None, :] <= query_pos[:, None]) & (seg_req[None, :] == s_blk[:, None])
        masked = jnp.where(seen, scores, MASK_LOW)
        top_score = lax.optimization_barrier(jnp.max(masked, axis=-1, keepdims=True))
        expo = jnp.where(seen, jnp.exp(masked - top_score), 0.0)
        total = lax.optimization_barrier(jnp.sum(expo, axis=-1))
        attn_weights = lax.optimization_barrier(expo.astype(jnp.bfloat16)).astype(jnp.float32)
        summed = jnp.einsum('kqij,jkd->kqid', attn_weights, value_all, precision=HIGH) / total[..., None]
        return summed.transpose(2, 0, 1, 3).reshape(TOK_DEV, QHEADS * HEAD_DIM).astype(jnp.bfloat16)
    outputs = lax.map(one_block, (q_blocks, s_blocks, starts))
    return outputs.reshape(WINDOW_LENGTH, QHEADS * HEAD_DIM)

def reference(mixer_input, gate_input, input_coeff, output_coeff, log_decay, skip_gain, norm_gain, segment_ids, query_rows, key_rows, value_rows, owner_map):

    def one_request(args):
        x_req, z_req, b_req, c_req, d_req, s_req, q_req, k_req, v_req = args
        ssd_mix, final_state = ssd_request(x_req, b_req, c_req, d_req, s_req, skip_gain)
        gated = lax.optimization_barrier(ssd_mix).astype(jnp.float32) * jax.nn.silu(z_req.astype(jnp.float32))
        grouped = gated.reshape(WINDOW_LENGTH, SSM_GROUPS, HEADS * HEAD_P // SSM_GROUPS)
        mean_sq = lax.optimization_barrier(jnp.mean(grouped * grouped, axis=2, keepdims=True))
        normed = (grouped * lax.rsqrt(mean_sq + NORM_EPS)).reshape(WINDOW_LENGTH, HEADS * HEAD_P)
        normed = (normed * norm_gain[None, :]).astype(jnp.bfloat16)
        attended = attend_request(q_req, k_req, v_req, s_req)
        return (normed, attended, final_state)
    mixer_output, attention_out, finals = lax.map(one_request, (mixer_input, gate_input, input_coeff, output_coeff, log_decay, segment_ids, query_rows, key_rows, value_rows))
    owner_grid = owner_map.reshape(REQUEST_COUNT, N_HEAD, N_POOL)
    slot_ids = jnp.arange(N_POOL)
    pick_table = jnp.where(owner_grid[:, :, None, :] == slot_ids[None, None, :, None], 1.0, 0.0).astype(jnp.float32)
    final_grid = finals.reshape(REQUEST_COUNT, N_HEAD, N_POOL, HEADS // (N_HEAD * N_POOL), HEAD_P, STATE)
    owned_states = jnp.einsum('rhog,rhgjpn->orhjpn', pick_table, final_grid, precision=HIGH)
    owned_states = owned_states.reshape(N_POOL, REQUEST_COUNT, HEADS // N_POOL, HEAD_P, STATE)

    def page_handover(rows_all):
        split_rows = rows_all.astype(jnp.float32).reshape(REQUEST_COUNT, N_SEQ, N_POOL, TOK_DEV // N_POOL, N_HEAD, KV_HEADS * HEAD_DIM // N_HEAD)
        moved = jnp.einsum('rhog,rsgihc->orsihc', pick_table, split_rows, precision=HIGH)
        return moved.reshape(N_POOL, REQUEST_COUNT, WINDOW_LENGTH // N_POOL, KV_HEADS * HEAD_DIM).astype(jnp.bfloat16)
    return (mixer_output, attention_out, owned_states, page_handover(key_rows), page_handover(value_rows))
```

```python
import functools
import math

import jax
import jax.numpy as jnp
from jax import lax
from jax.experimental import pallas as pl
from jax.experimental.pallas import tpu as pltpu
from jax.sharding import PartitionSpec as P

HEAD_P = 64
STATE = 256
HEAD_DIM = 128
NORM_EPS = 1e-05
HIGH = lax.Precision.HIGHEST
LOG2E = math.log2(math.e)
FAR = -1e30
F32 = jnp.float32
BF16 = jnp.bfloat16
MESH = pl.DeviceIdType.MESH
NN = (((1,), (0,)), ((), ()))
NT = (((1,), (1,)), ((), ()))


def mm(a, b, dims=NN, precision=None):
    return lax.dot_general(a, b, dims, precision=precision, preferred_element_type=F32)


def expand(parts, grid):
    high = parts.astype(BF16)
    rest = parts - high.astype(F32)
    middle = rest.astype(BF16)
    low = (rest - middle.astype(F32)).astype(BF16)
    return mm(high, grid) + mm(middle, grid) + mm(low, grid)


def kernel(
    n,
    n_pool,
    x_ref,
    z_ref,
    b_ref,
    c_ref,
    ld_ref,
    skip_ref,
    gain_ref,
    seg_ref,
    q_ref,
    k_ref,
    v_ref,
    own_ref,
    mix_out,
    att_out,
    st_out,
    ok_out,
    ov_out,
    s_f32,
    send1,
    recv1,
    send2,
    recv2,
    brief,
    kv,
    qa,
    run_max,
    run_sum,
    run_out,
    mix0,
    enter_x,
    silu_z,
    pages_k,
    pages_v,
    st_rows,
    st_send,
    sem_b,
    sem_1,
    sem_2,
    sem_kz,
    sem_kx,
    sem_pk,
    sem_pv,
    sem_ps,
):
    rows = x_ref.shape[1]
    chans = x_ref.shape[2]
    heads = ld_ref.shape[1]
    q_heads = q_ref.shape[2] // HEAD_DIM
    p_rows = HEAD_P // n
    side = math.isqrt(n)
    groups = n // side
    key_blk = 2 * rows
    blk_per_group = side // 2
    page_rows = rows // n_pool
    grp_heads = heads // n_pool
    me = lax.axis_index("seq")
    my_pool = lax.axis_index("pool")
    grp = me // side
    place = lax.rem(me, side)

    def remote(src, dst, sems, send_at, recv_at, axis, to):
        return pltpu.make_async_remote_copy(
            src_ref=src,
            dst_ref=dst,
            send_sem=sems.at[0, send_at],
            recv_sem=sems.at[1, recv_at],
            device_id={axis: to},
            device_id_type=MESH,
        )

    barrier = pltpu.get_barrier_semaphore()

    def greet(k, u):
        pl.semaphore_signal(
            barrier, inc=1, device_id={"seq": lax.rem(me + k, n)}, device_id_type=MESH
        )
        return u

    lax.fori_loop(1, n, greet, 0)
    for k in range(1, n_pool):
        pl.semaphore_signal(
            barrier, inc=1, device_id={"pool": lax.rem(my_pool + k, n_pool)}, device_id_type=MESH
        )

    row_i = lax.broadcasted_iota(jnp.int32, (rows, rows), 0)
    col_i = lax.broadcasted_iota(jnp.int32, (rows, rows), 1)
    lower = (col_i <= row_i).astype(F32)
    unit = (col_i == row_i).astype(F32)
    ld = ld_ref[0]
    cs = mm(ld, lower, NT, HIGH)
    cs_t = mm(lower, ld, NT, HIGH)
    seg_row = seg_ref[...].astype(F32)
    seg_rows = jnp.broadcast_to(seg_row, (8, rows))
    seg_col = mm(unit, seg_rows, NT)[:, 0:1]
    last_seg = seg_row[:, rows - 1 : rows]

    head_lane = jnp.concatenate(
        [jnp.exp(cs_t[rows - 1 : rows, :]), jnp.zeros((1, 128 - heads), F32)], axis=1
    )
    count_0 = jnp.sum(jnp.where(seg_row == 0.0, 1.0, 0.0), axis=1, keepdims=True)
    count_1 = jnp.sum(jnp.where(seg_row == 1.0, 1.0, 0.0), axis=1, keepdims=True)
    info = [head_lane] + [jnp.broadcast_to(v, (1, 128)) for v in (last_seg, count_0, count_1)]
    brief[me] = jnp.concatenate(info + [jnp.zeros((4, 128), F32)], axis=0)

    mine = pl.multiple_of(me * rows, rows)
    kv[pl.ds(mine, rows), 0:HEAD_DIM] = k_ref[0]
    kv[pl.ds(mine, rows), HEAD_DIM : 2 * HEAD_DIM] = v_ref[0]
    owners = own_ref[...]
    for src, dst in ((k_ref, pages_k), (v_ref, pages_v)):
        for o in range(n_pool):
            page = jnp.zeros((page_rows, HEAD_DIM), F32)
            for g in range(n_pool):
                part = src[0, g * page_rows : (g + 1) * page_rows, :].astype(F32)
                page = jnp.where(owners[:, g : g + 1] == o, part, page)
            dst[o] = page.astype(BF16)

    tail_w = jnp.where(seg_row == last_seg, jnp.exp(cs[:, rows - 1 : rows] - cs), 0.0)
    b_all = b_ref[0]
    for pair in range(heads // 2):
        x_t = x_ref[0, :, pair * 128 : pair * 128 + 128].astype(F32).T
        tail = [
            x_t[i * HEAD_P : (i + 1) * HEAD_P] * tail_w[2 * pair + i : 2 * pair + i + 1]
            for i in range(2)
        ]
        tail_x = jnp.concatenate(tail, axis=0).astype(BF16)
        state = mm(tail_x, b_all)
        for w in range(2):
            s_f32[w, pair * 128 : pair * 128 + 128, :] = state[:, w * 128 : w * 128 + 128]
    for s in range(n):
        for j in range(p_rows):
            for w in range(2):
                part = s_f32[w, pl.ds(s * p_rows + j, heads, stride=HEAD_P), :]
                send1[s, j * heads : (j + 1) * heads, w * 128 : w * 128 + 128] = part.astype(BF16)
    recv1[me] = send1[me]

    pl.semaphore_wait(barrier, n - 1 + n_pool - 1)

    def brief_copy(to, src):
        return remote(brief.at[me], brief.at[src], sem_b, to, src, "seq", to)

    def state_copy(to, src):
        return remote(send1.at[to], recv1.at[src], sem_1, to, src, "seq", to)

    def back_copy(to, src):
        return remote(send2.at[to], recv2.at[src], sem_2, to, src, "seq", to)

    def start_1(k, u):
        to = lax.rem(me + k, n)
        brief_copy(to, me).start()
        state_copy(to, me).start()
        return u

    lax.fori_loop(1, n, start_1, 0)

    def kz_copy(k, src):
        to = grp * side + lax.rem(place + k, side)
        at = pl.ds(pl.multiple_of(src * rows, rows), rows)
        return remote(kv.at[at], kv.at[at], sem_kz, k, k, "seq", to)

    for k in range(1, side):
        kz_copy(k, me).start()

    def pool_copies(k):
        to = lax.rem(my_pool + k, n_pool)
        return (
            remote(pages_k.at[to], ok_out.at[0, my_pool], sem_pk, k, k, "pool", to),
            remote(pages_v.at[to], ov_out.at[0, my_pool], sem_pv, k, k, "pool", to),
        )

    for k in range(1, n_pool):
        for c in pool_copies(k):
            c.start()
    ok_out[0, my_pool] = pages_k[my_pool]
    ov_out[0, my_pool] = pages_v[my_pool]

    head_of = lax.broadcasted_iota(jnp.int32, (heads, chans), 1) // HEAD_P
    grid = (head_of == lax.broadcasted_iota(jnp.int32, (heads, chans), 0)).astype(BF16)
    skip_x = expand(jnp.broadcast_to(skip_ref[...], (8, heads)), grid)[0:1]
    inner = mm(c_ref[0], b_all, NT)
    inner = jnp.where((col_i <= row_i) & (seg_col == seg_row), inner, 0.0)
    half = lax.broadcasted_iota(jnp.int32, (rows, 128), 1) < HEAD_P
    for pair in range(heads // 2):
        lanes = slice(pair * 128, pair * 128 + 128)
        x_pair = x_ref[0, :, lanes]
        y = []
        for h in (2 * pair, 2 * pair + 1):
            gap = jnp.minimum(cs_t[:, h : h + 1] - cs[h : h + 1, :], 0.0)
            y.append(mm((inner * jnp.exp(gap)).astype(BF16), x_pair))
        mix0[:, lanes] = jnp.where(half, y[0], y[1]) + skip_x[:, lanes] * x_pair.astype(F32)
        gate = z_ref[0, :, lanes].astype(F32)
        silu_z[:, lanes] = gate / (1.0 + jnp.exp(-gate))

    lane = lax.broadcasted_iota(jnp.int32, (rows, HEAD_DIM), 1).astype(F32)
    q_doc = jnp.where(lane == seg_col, 1.0, 0.0).astype(BF16)
    for a in range(q_heads):
        qa[a, :, 0:HEAD_DIM] = q_ref[0, :, a * HEAD_DIM : (a + 1) * HEAD_DIM]
        qa[a, :, HEAD_DIM : 2 * HEAD_DIM] = q_doc

    def brief_wait(k, u):
        src = lax.rem(me + k, n)
        brief_copy(src, src).wait_recv()
        return u

    lax.fori_loop(1, n, brief_wait, 0)
    all_brief = brief[...]
    factors = all_brief[:, 0, :]
    lasts = all_brief[:, 1, :]
    before = jnp.concatenate([jnp.full((1, 128), -1.0, F32), lasts[: n - 1]], axis=0)
    through = jnp.where(lasts == before, factors, 0.0)
    pick = lax.broadcasted_iota(jnp.int32, (heads, 128), 0) == lax.broadcasted_iota(
        jnp.int32, (heads, 128), 1
    )
    through_t = mm(pick.astype(F32), through, NT, HIGH)
    edge_0 = jnp.sum(all_brief[:, 2, :], axis=0, keepdims=True)
    edge_1 = edge_0 + jnp.sum(all_brief[:, 3, :], axis=0, keepdims=True)
    prev_last = brief[jnp.maximum(me - 1, 0)][1:2, 0:1]
    prev_last = jnp.where(me == 0, -1.0, prev_last)
    enter = jnp.where(seg_col == prev_last, jnp.exp(cs_t), 0.0)
    enter_x[...] = expand(enter, grid)

    for k in range(1, side):
        kz_copy(k, grp * side + lax.rem(place + side - k, side)).wait_recv()

    def kx_copy(to_grp, src_grp):
        at = pl.ds(pl.multiple_of(src_grp * side * rows, rows), side * rows)
        return remote(kv.at[at], kv.at[at], sem_kx, to_grp, src_grp, "seq", to_grp * side + place)

    for g in range(1, groups):

        @pl.when(grp < g)
        def _():
            kx_copy(g, grp).start()

    scale = HEAD_DIM ** (-0.5) * LOG2E
    blk_row = lax.broadcasted_iota(jnp.int32, (key_blk, HEAD_DIM), 0)
    blk_lane = lax.broadcasted_iota(jnp.int32, (key_blk, HEAD_DIM), 1)
    causal_key = lax.broadcasted_iota(jnp.int32, (rows, key_blk), 1)
    causal_row = lax.broadcasted_iota(jnp.int32, (rows, key_blk), 0)

    def attend(blk, first):
        at = pl.ds(pl.multiple_of(blk * key_blk, key_blk), key_blk)
        key_pos = (blk_row + blk * key_blk).astype(F32)
        doc = jnp.where(key_pos >= edge_0, 1, 0) + jnp.where(key_pos >= edge_1, 1, 0)
        k_doc = jnp.where((doc != blk_lane) & (blk_lane < 3), FAR, 0.0).astype(BF16)
        keys = jnp.concatenate([kv[at, 0:HEAD_DIM], k_doc], axis=1)
        values = kv[at, HEAD_DIM : 2 * HEAD_DIM]
        for a in range(q_heads):
            s = mm(qa[a], keys, NT)
            if first:
                seen = causal_key + blk * key_blk <= causal_row + me * rows
                s = jnp.where(seen, s, FAR)
            top = jnp.max(s, axis=1, keepdims=True)
            if not first:
                old = run_max[a]
                top = jnp.maximum(old[:, 0:1], top)
            e = jnp.exp2((s - top) * scale)
            total = sum(e[:, i : i + 128] for i in range(0, key_blk, 128))
            out = mm(e.astype(BF16), values)
            wide = jnp.broadcast_to(top, (rows, 128))
            if not first:
                shrink = jnp.exp2((old - wide) * scale)
                total = total + run_sum[a] * shrink
                out = out + run_out[a] * shrink
            run_max[a] = wide
            run_sum[a] = total
            run_out[a] = out

    own_blk = me // 2
    grp_blk = grp * blk_per_group
    attend(own_blk, True)

    def attend_own(i, u):
        attend(own_blk - 1 - i, False)
        return u

    lax.fori_loop(0, own_blk - grp_blk, attend_own, 0)

    @pl.when(me == 0)
    def _():
        recv2[...] = jnp.zeros_like(recv2)

    carry = [jnp.zeros((heads, STATE), F32) for _ in range(p_rows)]
    for c in range(n):
        if c > 0:
            for j in range(p_rows):
                send2[c, j * heads : (j + 1) * heads, :] = carry[j].astype(BF16)

            @pl.when(me == c)
            def _():
                recv2[c] = send2[c]

            @pl.when(me != c)
            def _():
                back_copy(c, me).start()

        @pl.when(me != c)
        def _():
            state_copy(c, c).wait_recv()

        keep = through_t[:, c : c + 1]
        for j in range(p_rows):
            part = recv1[c, j * heads : (j + 1) * heads, :].astype(F32)
            carry[j] = part if c == 0 else carry[j] * keep + part

    for o in range(n_pool):
        for j in range(p_rows):
            part = jnp.zeros((grp_heads, STATE), F32)
            for g in range(n_pool):
                given = carry[j][g * grp_heads : (g + 1) * grp_heads]
                part = jnp.where(owners[:, g : g + 1] == o, given, part)
            for w in range(2):
                st_rows[w, pl.ds(j, grp_heads, stride=p_rows), :] = part[:, w * 128 : w * 128 + 128]
        st_send[o] = jnp.concatenate([st_rows[0], st_rows[1]], axis=1)

    def st_copy(k):
        to = lax.rem(my_pool + k, n_pool)
        return remote(st_send.at[to], st_out.at[my_pool], sem_ps, k, k, "pool", to)

    for k in range(1, n_pool):
        st_copy(k).start()
    st_out[my_pool] = st_send[my_pool]

    for g in range(groups - 1):

        @pl.when(grp > g)
        def _():
            kx_copy(g, g).wait_recv()

    def attend_rest(i, u):
        attend(grp_blk - 1 - i, False)
        return u

    lax.fori_loop(0, grp_blk, attend_rest, 0)
    for a in range(q_heads):
        total = jnp.sum(run_sum[a], axis=1, keepdims=True)
        att_out[0, :, a * HEAD_DIM : (a + 1) * HEAD_DIM] = (run_out[a] / total).astype(BF16)

    for s in range(n):

        @pl.when((me > 0) & (me != s))
        def _():
            back_copy(s, s).wait_recv()

        for j in range(p_rows):
            part = recv2[s, j * heads : (j + 1) * heads, :].astype(F32)
            for w in range(2):
                spread = pl.ds(s * p_rows + j, heads, stride=HEAD_P)
                s_f32[w, spread, :] = part[:, w * 128 : w * 128 + 128]
    c_all = c_ref[0]
    square = jnp.zeros((rows, 128), F32)
    for at in range(0, chans, 256):
        lanes = slice(at, at + 256)
        state = jnp.concatenate([s_f32[0, lanes, :], s_f32[1, lanes, :]], axis=1)
        y = mm(c_all, state.astype(BF16), NT)
        mixed = (mix0[:, lanes] + y * enter_x[:, lanes]).astype(BF16).astype(F32)
        gated = mixed * silu_z[:, lanes]
        mix0[:, lanes] = gated
        square = square + gated[:, 0:128] * gated[:, 0:128] + gated[:, 128:] * gated[:, 128:]
    mean = jnp.sum(square, axis=1, keepdims=True) * (1.0 / chans)
    norm = lax.rsqrt(mean + NORM_EPS)
    for at in range(0, chans, 256):
        lanes = slice(at, at + 256)
        mix_out[0, :, lanes] = (mix0[:, lanes] * norm * gain_ref[:, lanes]).astype(BF16)

    def sent(k, u):
        to = lax.rem(me + k, n)
        brief_copy(to, me).wait_send()
        state_copy(to, me).wait_send()

        @pl.when(to > 0)
        def _():
            back_copy(to, me).wait_send()

        return u

    lax.fori_loop(1, n, sent, 0)
    for k in range(1, side):
        kz_copy(k, me).wait_send()
    for g in range(1, groups):

        @pl.when(grp < g)
        def _():
            kx_copy(g, grp).wait_send()

    for k in range(1, n_pool):
        for c in pool_copies(k) + (st_copy(k),):
            c.wait()


def local(n, n_pool, *args):
    (x, z, b, c, ld, skip, gain, seg, q, k, v, owner) = args
    rows, chans = x.shape[1:]
    heads = ld.shape[1]
    q_heads = q.shape[2] // HEAD_DIM
    p_rows = HEAD_P // n
    grp_heads = heads // n_pool
    page_rows = rows // n_pool
    vmem = pl.BlockSpec(memory_space=pltpu.VMEM)
    part = p_rows * heads
    pages = (n_pool, page_rows, HEAD_DIM)
    out = pl.pallas_call(
        functools.partial(kernel, n, n_pool),
        out_shape=(
            jax.ShapeDtypeStruct(x.shape, BF16),
            jax.ShapeDtypeStruct(q.shape, BF16),
            jax.ShapeDtypeStruct((n_pool, grp_heads * p_rows, STATE), F32),
            jax.ShapeDtypeStruct((1,) + pages, BF16),
            jax.ShapeDtypeStruct((1,) + pages, BF16),
        ),
        in_specs=[vmem] * 12,
        out_specs=[vmem] * 5,
        scratch_shapes=[
            pltpu.VMEM((2, chans, STATE // 2), F32),
            pltpu.VMEM((n, part, STATE), BF16),
            pltpu.VMEM((n, part, STATE), BF16),
            pltpu.VMEM((n, part, STATE), BF16),
            pltpu.VMEM((n, part, STATE), BF16),
            pltpu.VMEM((n, 8, 128), F32),
            pltpu.VMEM((n * rows, 2 * HEAD_DIM), BF16),
            pltpu.VMEM((q_heads, rows, 2 * HEAD_DIM), BF16),
            pltpu.VMEM((q_heads, rows, HEAD_DIM), F32),
            pltpu.VMEM((q_heads, rows, HEAD_DIM), F32),
            pltpu.VMEM((q_heads, rows, HEAD_DIM), F32),
            pltpu.VMEM((rows, chans), F32),
            pltpu.VMEM((rows, chans), F32),
            pltpu.VMEM((rows, chans), F32),
            pltpu.VMEM(pages, BF16),
            pltpu.VMEM(pages, BF16),
            pltpu.VMEM((2, grp_heads * p_rows, STATE // 2), F32),
            pltpu.VMEM((n_pool, grp_heads * p_rows, STATE), F32),
            pltpu.SemaphoreType.DMA((2, n)),
            pltpu.SemaphoreType.DMA((2, n)),
            pltpu.SemaphoreType.DMA((2, n)),
            pltpu.SemaphoreType.DMA((2, n)),
            pltpu.SemaphoreType.DMA((2, n)),
            pltpu.SemaphoreType.DMA((2, n)),
            pltpu.SemaphoreType.DMA((2, n)),
            pltpu.SemaphoreType.DMA((2, n)),
        ],
        compiler_params=pltpu.CompilerParams(
            collective_id=0, has_side_effects=True, vmem_limit_bytes=50 * 1024 * 1024
        ),
    )(x, z, b, c, ld, skip.reshape(1, -1), gain.reshape(1, -1), seg, q, k, v, owner)
    mixer, attended, states, keys, values = out
    return mixer, attended, states.reshape(1, n_pool, grp_heads, p_rows, STATE), keys, values


def solution(mesh):
    return jax.shard_map(
        functools.partial(local, mesh.shape["seq"], mesh.shape["pool"]),
        mesh=mesh,
        in_specs=(
            P("pool", "seq", "head"),
            P("pool", "seq", "head"),
            P("pool", "seq", "head"),
            P("pool", "seq", "head"),
            P("pool", "head", "seq"),
            P("head"),
            P("head"),
            P("pool", "seq"),
            P("pool", "seq", "head"),
            P("pool", "seq", "head"),
            P("pool", "seq", "head"),
            P("pool", "head"),
        ),
        out_specs=(
            P("pool", "seq", "head"),
            P("pool", "seq", "head"),
            P("pool", None, "head", "seq", None),
            P("pool", None, "seq", "head"),
            P("pool", None, "seq", "head"),
        ),
        check_vma=False,
    )
```

```python
import functools
import math

import jax
import jax.numpy as jnp
from jax import lax
from jax.experimental import pallas as pl
from jax.experimental.pallas import tpu as pltpu
from jax.sharding import PartitionSpec as P

HEAD_P = 64
STATE = 256
HEAD_DIM = 128
NORM_EPS = 1e-05
HIGH = lax.Precision.HIGHEST
LOG2E = math.log2(math.e)
FAR = -1e30
F32 = jnp.float32
BF16 = jnp.bfloat16
MESH = pl.DeviceIdType.MESH
NN = (((1,), (0,)), ((), ()))
NT = (((1,), (1,)), ((), ()))


def mm(a, b, dims=NN, precision=None):
    return lax.dot_general(a, b, dims, precision=precision, preferred_element_type=F32)


def expand(parts, grid):
    high = parts.astype(BF16)
    rest = parts - high.astype(F32)
    middle = rest.astype(BF16)
    low = (rest - middle.astype(F32)).astype(BF16)
    return mm(high, grid) + mm(middle, grid) + mm(low, grid)


def split_two(parts):
    high = parts.astype(BF16)
    return jnp.concatenate([high, (parts - high.astype(F32)).astype(BF16)], axis=1)


def kernel(
    n,
    n_pool,
    x_hbm,
    z_hbm,
    b_hbm,
    c_hbm,
    ld_hbm,
    skip_hbm,
    gain_hbm,
    seg_hbm,
    q_hbm,
    k_hbm,
    v_hbm,
    own_hbm,
    mix_out,
    att_out,
    st_out,
    ok_out,
    ov_out,
    mix_v,
    att_v,
    x_ref,
    z_ref,
    b_ref,
    c_ref,
    ld_ref,
    skip_ref,
    gain_ref,
    seg_ref,
    own_ref,
    qa,
    kv,
    send1,
    recv1,
    sums,
    others,
    send2,
    recv2,
    brief,
    factor,
    score,
    run_max,
    run_sum,
    run_out,
    mix0,
    enter_x,
    silu_z,
    pages_k,
    pages_v,
    fin,
    fin_t,
    fin_send,
    fin_recv,
    st_send,
    sem_in,
    sem_out,
    sem_b,
    sem_1,
    sem_p,
    sem_2,
    sem_f,
    sem_kz,
    sem_kx,
    sem_pool,
):
    rows = x_hbm.shape[1]
    chans = x_hbm.shape[2]
    heads = ld_hbm.shape[1]
    q_heads = q_hbm.shape[2] // HEAD_DIM
    p_rows = HEAD_P // n
    n_rows = STATE // n
    side = math.isqrt(n)
    groups = n // side
    inner_n = side // 2
    owners_n = groups * inner_n
    span = side * rows
    page_rows = rows // n_pool
    grp_heads = heads // n_pool
    tiles = chans // 128
    me = lax.axis_index("seq")
    my_pool = lax.axis_index("pool")
    grp = me // side
    place = lax.rem(me, side)
    half = place // inner_n
    mine_o = grp * inner_n + lax.rem(place, inner_n)
    mine = pl.multiple_of(me * rows, rows)

    def remote(src, dst, send_sem, recv_sem, axis, to):
        return pltpu.make_async_remote_copy(
            src_ref=src,
            dst_ref=dst,
            send_sem=send_sem,
            recv_sem=recv_sem,
            device_id={axis: to},
            device_id_type=MESH,
        )

    own_rows = pl.ds(mine, rows)
    pairs = [
        (ld_hbm.at[0], ld_ref),
        (seg_hbm, seg_ref),
        (b_hbm.at[0], b_ref),
        (x_hbm.at[0], x_ref),
        (k_hbm.at[0], kv.at[own_rows, pl.ds(0, HEAD_DIM)]),
        (v_hbm.at[0], kv.at[own_rows, pl.ds(HEAD_DIM, HEAD_DIM)]),
        (own_hbm, own_ref),
        (c_hbm.at[0], c_ref),
        (skip_hbm, skip_ref),
        (z_hbm.at[0], z_ref),
        (gain_hbm, gain_ref),
    ] + [
        (
            q_hbm.at[0, :, pl.ds(a * HEAD_DIM, HEAD_DIM)],
            qa.at[pl.ds(a * rows, rows), pl.ds(0, HEAD_DIM)],
        )
        for a in range(q_heads)
    ]
    loads = [pltpu.make_async_copy(s, d, sem_in.at[i]) for i, (s, d) in enumerate(pairs)]
    for load in loads:
        load.start()

    barrier = pltpu.get_barrier_semaphore()

    def greet(k, u):
        pl.semaphore_signal(
            barrier, inc=1, device_id={"seq": lax.rem(me + k, n)}, device_id_type=MESH
        )
        return u

    lax.fori_loop(1, n, greet, 0)
    for k in range(1, n_pool):
        pl.semaphore_signal(
            barrier, inc=1, device_id={"pool": lax.rem(my_pool + k, n_pool)}, device_id_type=MESH
        )

    row_i = lax.broadcasted_iota(jnp.int32, (rows, rows), 0)
    col_i = lax.broadcasted_iota(jnp.int32, (rows, rows), 1)
    lower = (col_i <= row_i).astype(F32)
    unit = (col_i == row_i).astype(F32)
    head_of = lax.broadcasted_iota(jnp.int32, (heads, chans), 1) // HEAD_P
    grid = (head_of == lax.broadcasted_iota(jnp.int32, (heads, chans), 0)).astype(BF16)
    grid_two = jnp.concatenate([grid, grid], axis=0)
    for load in loads[:4]:
        load.wait()
    ld = ld_ref[...]
    cs = mm(ld, lower, NT, HIGH)
    cs_t = mm(lower, ld, NT, HIGH)
    seg_row = seg_ref[...].astype(F32)
    seg_rows = jnp.broadcast_to(seg_row, (8, rows))
    seg_col = mm(unit, seg_rows, NT)[:, 0:1]
    last_seg = seg_row[:, rows - 1 : rows]

    head_lane = jnp.concatenate(
        [jnp.exp(cs_t[rows - 1 : rows, :]), jnp.zeros((1, 128 - heads), F32)], axis=1
    )
    count_0 = jnp.sum(jnp.where(seg_row == 0.0, 1.0, 0.0), axis=1, keepdims=True)
    count_1 = jnp.sum(jnp.where(seg_row == 1.0, 1.0, 0.0), axis=1, keepdims=True)
    info = [head_lane] + [jnp.broadcast_to(v, (1, 128)) for v in (last_seg, count_0, count_1)]
    brief[me] = jnp.concatenate(info + [jnp.zeros((4, 128), F32)], axis=0)

    tail_w = jnp.where(seg_col == last_seg, jnp.exp(cs_t[rows - 1 : rows, :] - cs_t), 0.0)
    tail_two = split_two(tail_w)
    b_t = b_ref[...].astype(F32).T.astype(BF16)
    for at in range(0, chans, 256):
        lanes = slice(at, at + 256)
        tail_x = (x_ref[:, lanes].astype(F32) * mm(tail_two, grid_two[:, lanes])).astype(BF16)
        state = mm(b_t, tail_x).astype(BF16)
        for s in range(n):
            send1[s // 2, s % 2, :, lanes] = state[s * n_rows : (s + 1) * n_rows]

    pl.semaphore_wait(barrier, n - 1 + n_pool - 1)

    def peer(o):
        return (o // inner_n) * side + half * inner_n + lax.rem(o, inner_n)

    def own_copy(k, o, src):
        return remote(
            send1.at[o, k], recv1.at[src, k], sem_1.at[0, k, o], sem_1.at[1, k, src], "seq", peer(o)
        )

    def brief_copy(to, src):
        return remote(
            brief.at[me], brief.at[src], sem_b.at[0, to], sem_b.at[1, src], "seq", to
        )

    def kz_copy(k, src):
        to = grp * side + lax.rem(place + k, side)
        at = pl.ds(pl.multiple_of(src * rows, rows), rows)
        return remote(kv.at[at], kv.at[at], sem_kz.at[0, k], sem_kz.at[1, k], "seq", to)

    for k in range(2):

        def start_own(i, u, k=k):
            own_copy(k, lax.rem(mine_o + i, owners_n), mine_o).start()
            return u

        lax.fori_loop(1, owners_n, start_own, 0)

    def start_brief(i, u):
        brief_copy(lax.rem(me + i, n), me).start()
        return u

    lax.fori_loop(1, n, start_brief, 0)
    for load in loads[4:6]:
        load.wait()
    for k in range(1, side):
        kz_copy(k, me).start()
    for k in range(2):
        recv1[mine_o, k] = send1[mine_o, k]

    loads[6].wait()
    owners = own_ref[...]
    for w, pages in ((0, pages_k), (1, pages_v)):
        for o in range(n_pool):
            page = jnp.zeros((page_rows, HEAD_DIM), F32)
            for g in range(n_pool):
                at = pl.ds(pl.multiple_of(mine + g * page_rows, 16), page_rows)
                part = kv[at, w * HEAD_DIM : (w + 1) * HEAD_DIM].astype(F32)
                page = jnp.where(owners[:, g : g + 1] == o, part, page)
            pages[o] = page.astype(BF16)

    def pool_copy(k, which):
        to = lax.rem(my_pool + k, n_pool)
        src, dst = ((pages_k, ok_out.at[0]), (pages_v, ov_out.at[0]), (st_send, st_out))[which]
        return remote(
            src.at[to],
            dst.at[my_pool],
            sem_pool.at[0, which, k],
            sem_pool.at[1, which, k],
            "pool",
            to,
        )

    for k in range(1, n_pool):
        for which in range(2):
            pool_copy(k, which).start()
    stores = [
        pltpu.make_async_copy(pages_k.at[my_pool], ok_out.at[0, my_pool], sem_out.at[0]),
        pltpu.make_async_copy(pages_v.at[my_pool], ov_out.at[0, my_pool], sem_out.at[1]),
        pltpu.make_async_copy(st_send.at[my_pool], st_out.at[my_pool], sem_out.at[2]),
        pltpu.make_async_copy(att_v, att_out.at[0], sem_out.at[3]),
    ]
    stores[0].start()
    stores[1].start()

    def brief_wait(i, u):
        src = lax.rem(me + i, n)
        brief_copy(src, src).wait_recv()
        return u

    lax.fori_loop(1, n, brief_wait, 0)
    all_brief = brief[...]
    lasts = all_brief[:, 1, :]
    before = jnp.concatenate([jnp.full((1, 128), -1.0, F32), lasts[: n - 1]], axis=0)
    through = jnp.where(lasts == before, all_brief[:, 0, :], 0.0)
    line = [through[c : c + 1] for c in range(n)]
    run = [
        [math.prod(line[g * side + h * inner_n + i] for i in range(inner_n)) for g in range(groups)]
        for h in range(2)
    ]
    table = [jnp.where(half == 0, run[1][max(g - 1, 0)], run[0][g]) for g in range(groups)]
    for g in range(groups):
        for i in range(inner_n):
            a, b = line[g * side + i], line[g * side + inner_n + i]
            table.append(jnp.where(half == 0, a, b))
    table.append(run[1][groups - 1])
    end_at = len(table) - 1
    table = jnp.concatenate(table + [jnp.zeros((16 - len(table), 128), F32)], axis=0)
    factor[...] = expand(table[:, 0:heads], grid)
    edge_0 = jnp.sum(all_brief[:, 2, :], axis=0, keepdims=True)
    edge_1 = edge_0 + jnp.sum(all_brief[:, 3, :], axis=0, keepdims=True)
    prev_last = brief[jnp.maximum(me - 1, 0)][1:2, 0:1]
    prev_last = jnp.where(me == 0, -1.0, prev_last)
    enter_two = split_two(jnp.where(seg_col == prev_last, jnp.exp(cs_t), 0.0))

    for load in loads[7:]:
        load.wait()
    skip_x = expand(jnp.broadcast_to(skip_ref[...], (8, heads)), grid)[0:1]
    inner = mm(c_ref[...], b_t)
    inner = jnp.where((col_i <= row_i) & (seg_col == seg_row), inner, 0.0)
    first_half = lax.broadcasted_iota(jnp.int32, (rows, 128), 1) < HEAD_P

    def within(pair):
        lanes = slice(pair * 128, pair * 128 + 128)
        x_pair = x_ref[:, lanes]
        y = []
        for h in (2 * pair, 2 * pair + 1):
            gap = jnp.minimum(cs_t[:, h : h + 1] - cs[h : h + 1, :], 0.0)
            y.append(mm((inner * jnp.exp(gap)).astype(BF16), x_pair))
        mix0[:, lanes] = jnp.where(first_half, y[0], y[1]) + skip_x[:, lanes] * x_pair.astype(F32)
        gate = z_ref[:, lanes].astype(F32)
        silu_z[:, lanes] = gate / (1.0 + jnp.exp(-gate))
        enter_x[:, lanes] = mm(enter_two, grid_two[:, lanes])

    for pair in range(heads // 2):
        within(pair)

    def sum_copy(k):
        to = grp * side + (1 - half) * inner_n + lax.rem(place, inner_n)
        return remote(
            sums.at[k],
            others.at[k, pl.ds(1, groups)],
            sem_p.at[0, k],
            sem_p.at[1, k],
            "seq",
            to,
        )

    for k in range(2):

        def wait_own(i, u, k=k):
            o = lax.rem(mine_o + i, owners_n)
            own_copy(k, o, o).wait_recv()
            return u

        lax.fori_loop(1, owners_n, wait_own, 0)
        for g in range(groups):
            total = recv1[g * inner_n, k].astype(F32)
            for i in range(1, inner_n):
                at = groups + g * inner_n + i
                total = total * factor[at : at + 1, :] + recv1[g * inner_n + i, k].astype(F32)
            sums[k, g] = total.astype(BF16)
        sum_copy(k).start()

    lane = lax.broadcasted_iota(jnp.int32, (rows, HEAD_DIM), 1).astype(F32)
    q_doc = jnp.where(lane == seg_col, 1.0, 0.0).astype(BF16)
    for a in range(q_heads):
        qa[a * rows : (a + 1) * rows, HEAD_DIM : 2 * HEAD_DIM] = q_doc

    for k in range(1, side):
        kz_copy(k, grp * side + lax.rem(place + side - k, side)).wait_recv()

    def kx_copy(to_grp, src_grp):
        at = pl.ds(pl.multiple_of(src_grp * span, span), span)
        to = to_grp * side + place
        return remote(
            kv.at[at], kv.at[at], sem_kx.at[0, to_grp], sem_kx.at[1, src_grp], "seq", to
        )

    for g in range(1, groups):

        @pl.when(grp < g)
        def _():
            kx_copy(g, grp).start()

    scale = HEAD_DIM ** (-0.5) * LOG2E
    key_lane = lax.broadcasted_iota(jnp.int32, (HEAD_DIM, span), 1)
    doc_row = lax.broadcasted_iota(jnp.int32, (HEAD_DIM, span), 0)
    causal_key = lax.broadcasted_iota(jnp.int32, (rows, span), 1)
    causal_row = lax.broadcasted_iota(jnp.int32, (rows, span), 0)
    edges = [jnp.concatenate([e] * (span // 128), axis=1) for e in (edge_0, edge_1)]

    def attend(g, first):
        at = pl.ds(pl.multiple_of(g * span, span), span)
        key_pos = (key_lane + g * span).astype(F32)
        doc = jnp.where(key_pos >= edges[0], 1, 0) + jnp.where(key_pos >= edges[1], 1, 0)
        k_doc = jnp.where((doc != doc_row) & (doc_row < 3), FAR, 0.0).astype(BF16)
        k_t = kv[at, 0:HEAD_DIM].astype(F32).T.astype(BF16)
        keys = jnp.concatenate([k_t, k_doc], axis=0)
        for a in range(q_heads):
            own = slice(a * rows, (a + 1) * rows)
            s = mm(qa[own, :], keys)
            if first:
                s = jnp.where(causal_key + g * span <= causal_row + me * rows, s, FAR)
            score[own, :] = s
            top = functools.reduce(jnp.maximum, [s[:, i : i + 128] for i in range(0, span, 128)])
            if not first:
                top = jnp.maximum(top, run_max[own])
            top = jnp.broadcast_to(jnp.max(top, axis=1, keepdims=True), (rows, 128))
            if not first:
                shrink = jnp.exp2((run_max[own] - top) * scale)
                run_sum[own] = run_sum[own] * shrink
                run_out[own] = run_out[own] * shrink
            run_max[own] = top
        values = kv[at, HEAD_DIM : 2 * HEAD_DIM]
        for a in range(q_heads):
            own = slice(a * rows, (a + 1) * rows)
            top = run_max[own]
            total = None if first else run_sum[own]
            weights = []
            for i in range(0, span, 128):
                e = jnp.exp2((score[own, i : i + 128] - top) * scale)
                total = e if total is None else total + e
                weights.append(e.astype(BF16))
            out = mm(jnp.concatenate(weights, axis=1), values)
            run_sum[own] = total
            run_out[own] = out if first else run_out[own] + out

    attend(grp, True)

    others[:, 0] = jnp.zeros_like(others[:, 0])

    def back_copy(k, o, src):
        return remote(
            send2.at[o, k], recv2.at[src, k], sem_2.at[0, k, o], sem_2.at[1, k, src], "seq", peer(o)
        )

    for k in range(2):
        sum_copy(k).wait_recv()
        carry = jnp.zeros((n_rows, chans), F32)
        for g in range(groups):
            carry = carry * factor[g : g + 1, :] + others[k, g + half].astype(F32)
            for i in range(inner_n):
                o = g * inner_n + i
                send2[o, k] = carry.astype(BF16)
                at = groups + o
                carry = carry * factor[at : at + 1, :] + recv1[o, k].astype(F32)

        def start_back(i, u, k=k):
            back_copy(k, lax.rem(mine_o + i, owners_n), mine_o).start()
            return u

        lax.fori_loop(1, owners_n, start_back, 0)
        recv2[mine_o, k] = send2[mine_o, k]

        @pl.when(half == k)
        def _():
            if k == 0:
                last = factor[end_at : end_at + 1, :]
                fin[...] = carry * last + others[k, groups].astype(F32)
            else:
                fin[...] = carry

    block_at = 2 * mine_o + half
    stacked = jnp.concatenate([fin[:, t * 128 : (t + 1) * 128] for t in range(tiles)], axis=0)
    fin_t[...] = stacked.T
    for s in range(n):
        for w in range(2):
            at = w * HEAD_P + s * p_rows
            fin_send[s, w * p_rows : (w + 1) * p_rows, :] = fin_t[at : at + p_rows, :]

    def fin_copy(to, src_block):
        return remote(
            fin_send.at[to],
            fin_recv.at[src_block],
            sem_f.at[0, to],
            sem_f.at[1, src_block],
            "seq",
            to,
        )

    def start_fin(i, u):
        fin_copy(lax.rem(me + i, n), block_at).start()
        return u

    lax.fori_loop(1, n, start_fin, 0)
    fin_recv[block_at] = fin_send[me]

    for g in range(groups - 1):

        @pl.when(grp > g)
        def _():
            kx_copy(g, g).wait_recv()

    def attend_rest(i, u):
        attend(grp - 1 - i, False)
        return u

    lax.fori_loop(0, grp, attend_rest, 0)
    for a in range(q_heads):
        own = slice(a * rows, (a + 1) * rows)
        total = jnp.sum(run_sum[own], axis=1, keepdims=True)
        att_v[:, a * HEAD_DIM : (a + 1) * HEAD_DIM] = (run_out[own] / total).astype(BF16)
    stores[3].start()

    def wait_fin(i, u):
        src = lax.rem(block_at + i, n)
        fin_copy(me, src).wait_recv()
        return u

    lax.fori_loop(1, n, wait_fin, 0)
    last = [
        jnp.concatenate(
            [fin_recv[s, :, t * n_rows : (t + 1) * n_rows] for s in range(n)], axis=1
        )
        for t in range(tiles)
    ]
    per = tiles // n_pool
    for o in range(n_pool):
        for t in range(per):
            part = jnp.zeros_like(last[0])
            for g in range(n_pool):
                part = jnp.where(owners[:, g : g + 1] == o, last[g * per + t], part)
            for w in range(2):
                st_send[o, 2 * t + w] = part[w * p_rows : (w + 1) * p_rows]
    for k in range(1, n_pool):
        pool_copy(k, 2).start()
    stores[2].start()

    for k in range(2):

        def sent(i, u, k=k):
            o = lax.rem(mine_o + i, owners_n)
            own_copy(k, o, mine_o).wait_send()
            back_copy(k, o, mine_o).wait_send()
            return u

        lax.fori_loop(1, owners_n, sent, 0)
        sum_copy(k).wait_send()

    def sent_all(i, u):
        to = lax.rem(me + i, n)
        brief_copy(to, me).wait_send()
        fin_copy(to, block_at).wait_send()
        return u

    lax.fori_loop(1, n, sent_all, 0)
    for k in range(1, side):
        kz_copy(k, me).wait_send()
    for g in range(1, groups):

        @pl.when(grp < g)
        def _():
            kx_copy(g, grp).wait_send()

    for k in range(1, n_pool):
        for which in range(2):
            pool_copy(k, which).wait()

    for k in range(2):

        def wait_back(i, u, k=k):
            o = lax.rem(mine_o + i, owners_n)
            back_copy(k, o, o).wait_recv()
            return u

        lax.fori_loop(1, owners_n, wait_back, 0)
    c_all = c_ref[...]
    square = jnp.zeros((rows, 128), F32)
    for at in range(0, chans, 256):
        lanes = slice(at, at + 256)
        entered = jnp.concatenate([recv2[s // 2, s % 2, :, lanes] for s in range(n)], axis=0)
        y = mm(c_all, entered)
        mixed = (mix0[:, lanes] + y * enter_x[:, lanes]).astype(BF16).astype(F32)
        gated = mixed * silu_z[:, lanes]
        mix0[:, lanes] = gated
        square = square + gated[:, 0:128] * gated[:, 0:128] + gated[:, 128:] * gated[:, 128:]
    mean = jnp.sum(square, axis=1, keepdims=True) * (1.0 / chans)
    norm = lax.rsqrt(mean + NORM_EPS)
    part = chans // 4
    for at in range(0, chans, 256):
        lanes = slice(at, at + 256)
        mix_v[:, lanes] = (mix0[:, lanes] * norm * gain_ref[:, lanes]).astype(BF16)
        if (at + 256) % part == 0:
            done = pl.ds(at + 256 - part, part)
            store = pltpu.make_async_copy(
                mix_v.at[:, done], mix_out.at[0, :, done], sem_out.at[4 + at // part]
            )
            store.start()
            stores.append(store)
    for k in range(1, n_pool):
        pool_copy(k, 2).wait()
    for store in stores:
        store.wait()


def store(*refs):
    count = (len(refs) - 1) // 2
    sem = refs[-1]
    copies = [
        pltpu.make_async_copy(refs[i], refs[count + i], sem.at[i]) for i in range(count)
    ]
    for copy in copies:
        copy.start()
    for copy in copies:
        copy.wait()


def local(n, n_pool, *args):
    (x, z, b, c, ld, skip, gain, seg, q, k, v, owner) = args
    rows, chans = x.shape[1:]
    heads = ld.shape[1]
    q_heads = q.shape[2] // HEAD_DIM
    p_rows = HEAD_P // n
    n_rows = STATE // n
    side = math.isqrt(n)
    groups = n // side
    owners_n = n // 2
    grp_heads = heads // n_pool
    page_rows = rows // n_pool
    tiles = chans // 128
    hbm = pl.BlockSpec(memory_space=pltpu.HBM)
    pages = (n_pool, page_rows, HEAD_DIM)
    states = (n_pool, grp_heads, p_rows, STATE)
    part = (owners_n, 2, n_rows, chans)
    dma = pltpu.SemaphoreType.DMA
    out = pl.pallas_call(
        functools.partial(kernel, n, n_pool),
        out_shape=(
            jax.ShapeDtypeStruct(x.shape, BF16),
            jax.ShapeDtypeStruct(q.shape, BF16),
            jax.ShapeDtypeStruct(states, F32),
            jax.ShapeDtypeStruct((1,) + pages, BF16),
            jax.ShapeDtypeStruct((1,) + pages, BF16),
        ),
        in_specs=[hbm] * 12,
        out_specs=[hbm] * 5,
        scratch_shapes=[
            pltpu.VMEM((rows, chans), BF16),
            pltpu.VMEM((rows, q_heads * HEAD_DIM), BF16),
            pltpu.VMEM((rows, chans), BF16),
            pltpu.VMEM((rows, chans), BF16),
            pltpu.VMEM((rows, STATE), BF16),
            pltpu.VMEM((rows, STATE), BF16),
            pltpu.VMEM((heads, rows), F32),
            pltpu.VMEM((1, heads), F32),
            pltpu.VMEM((1, chans), F32),
            pltpu.VMEM((1, rows), jnp.int32),
            pltpu.VMEM((1, n_pool), jnp.int32),
            pltpu.VMEM((q_heads * rows, 2 * HEAD_DIM), BF16),
            pltpu.VMEM((n * rows, 2 * HEAD_DIM), BF16),
            pltpu.VMEM(part, BF16),
            pltpu.VMEM(part, BF16),
            pltpu.VMEM((2, groups, n_rows, chans), BF16),
            pltpu.VMEM((2, groups + 1, n_rows, chans), BF16),
            pltpu.VMEM(part, BF16),
            pltpu.VMEM(part, BF16),
            pltpu.VMEM((n, 8, 128), F32),
            pltpu.VMEM((16, chans), F32),
            pltpu.VMEM((q_heads * rows, side * rows), F32),
            pltpu.VMEM((q_heads * rows, 128), F32),
            pltpu.VMEM((q_heads * rows, 128), F32),
            pltpu.VMEM((q_heads * rows, HEAD_DIM), F32),
            pltpu.VMEM((rows, chans), F32),
            pltpu.VMEM((rows, chans), F32),
            pltpu.VMEM((rows, chans), F32),
            pltpu.VMEM(pages, BF16),
            pltpu.VMEM(pages, BF16),
            pltpu.VMEM((n_rows, chans), F32),
            pltpu.VMEM((128, tiles * n_rows), F32),
            pltpu.VMEM((n, 2 * p_rows, tiles * n_rows), F32),
            pltpu.VMEM((n, 2 * p_rows, tiles * n_rows), F32),
            pltpu.VMEM(states, F32),
            dma((11 + q_heads,)),
            dma((8,)),
            dma((2, n)),
            dma((2, 2, owners_n)),
            dma((2, 2)),
            dma((2, 2, owners_n)),
            dma((2, n)),
            dma((2, side)),
            dma((2, groups)),
            dma((2, 3, n_pool)),
        ],
        compiler_params=pltpu.CompilerParams(
            collective_id=0, has_side_effects=True, vmem_limit_bytes=60 * 1024 * 1024
        ),
    )(x, z, b, c, ld, skip.reshape(1, -1), gain.reshape(1, -1), seg, q, k, v, owner)
    out = pl.pallas_call(
        store,
        out_shape=tuple(jax.ShapeDtypeStruct(o.shape, o.dtype) for o in out),
        in_specs=[hbm] * 5,
        out_specs=[hbm] * 5,
        scratch_shapes=[dma((5,))],
        compiler_params=pltpu.CompilerParams(vmem_limit_bytes=60 * 1024 * 1024),
    )(*out)
    mixer, attended, owned, keys, values = out
    return mixer, attended, owned[None], keys, values


def solution(mesh):
    return jax.shard_map(
        functools.partial(local, mesh.shape["seq"], mesh.shape["pool"]),
        mesh=mesh,
        in_specs=(
            P("pool", "seq", "head"),
            P("pool", "seq", "head"),
            P("pool", "seq", "head"),
            P("pool", "seq", "head"),
            P("pool", "head", "seq"),
            P("head"),
            P("head"),
            P("pool", "seq"),
            P("pool", "seq", "head"),
            P("pool", "seq", "head"),
            P("pool", "seq", "head"),
            P("pool", "head"),
        ),
        out_specs=(
            P("pool", "seq", "head"),
            P("pool", "seq", "head"),
            P("pool", None, "head", "seq", None),
            P("pool", None, "seq", "head"),
            P("pool", None, "seq", "head"),
        ),
        check_vma=False,
    )
```

```python
import functools
import math

import jax
import jax.numpy as jnp
from jax import lax
from jax.experimental import pallas as pl
from jax.experimental.pallas import tpu as pltpu
from jax.sharding import PartitionSpec as P

HEAD_P = 64
STATE = 256
HEAD_DIM = 128
NORM_EPS = 1e-05
HIGH = lax.Precision.HIGHEST
LOG2E = math.log2(math.e)
FAR = -1e30
F32 = jnp.float32
BF16 = jnp.bfloat16
MESH = pl.DeviceIdType.MESH
NN = (((1,), (0,)), ((), ()))
NT = (((1,), (1,)), ((), ()))


def mm(a, b, dims=NN, precision=None):
    return lax.dot_general(a, b, dims, precision=precision, preferred_element_type=F32)


def expand(parts, grid):
    high = parts.astype(BF16)
    rest = parts - high.astype(F32)
    middle = rest.astype(BF16)
    low = (rest - middle.astype(F32)).astype(BF16)
    return mm(high, grid) + mm(middle, grid) + mm(low, grid)


def split_two(parts):
    high = parts.astype(BF16)
    return jnp.concatenate([high, (parts - high.astype(F32)).astype(BF16)], axis=1)


def kernel(
    n,
    n_pool,
    x_hbm,
    z_hbm,
    b_hbm,
    c_hbm,
    ld_hbm,
    skip_hbm,
    gain_hbm,
    seg_hbm,
    q_hbm,
    k_hbm,
    v_hbm,
    own_hbm,
    mix_out,
    att_out,
    st_out,
    ok_out,
    ov_out,
    mix_v,
    att_v,
    x_ref,
    z_ref,
    b_ref,
    c_ref,
    ld_ref,
    skip_ref,
    gain_ref,
    seg_ref,
    own_ref,
    qa,
    kv,
    send1,
    recv1,
    sums,
    others,
    send2,
    recv2,
    brief,
    factor,
    score,
    run_max,
    run_sum,
    run_out,
    mix0,
    enter_x,
    silu_z,
    pages,
    fin_t,
    fin_send,
    fin_recv,
    st_send,
    sem_in,
    sem_out,
    sem_b,
    sem_1,
    sem_p,
    sem_2,
    sem_f,
    sem_kz,
    sem_kx,
    sem_pool,
):
    rows = x_hbm.shape[1]
    chans = x_hbm.shape[2]
    heads = ld_hbm.shape[1]
    q_heads = q_hbm.shape[2] // HEAD_DIM
    p_rows = HEAD_P // n
    n_rows = STATE // n
    side = math.isqrt(n)
    groups = n // side
    inner_n = side // 2
    owners_n = groups * inner_n
    half_chans = chans // 2
    chunks = 4
    span = side * rows
    page_rows = rows // n_pool
    grp_heads = heads // n_pool
    tiles = chans // 128
    me = lax.axis_index("seq")
    my_pool = lax.axis_index("pool")
    grp = me // side
    place = lax.rem(me, side)
    half = place // inner_n
    mine_o = grp * inner_n + lax.rem(place, inner_n)
    mine = pl.multiple_of(me * rows, rows)

    def remote(src, dst, send_sem, recv_sem, axis, to):
        return pltpu.make_async_remote_copy(
            src_ref=src,
            dst_ref=dst,
            send_sem=send_sem,
            recv_sem=recv_sem,
            device_id={axis: to},
            device_id_type=MESH,
        )

    own_rows = pl.ds(mine, rows)
    pairs = [
        (ld_hbm.at[0], ld_ref),
        (seg_hbm, seg_ref),
        (k_hbm.at[0], kv.at[own_rows, pl.ds(0, HEAD_DIM)]),
        (v_hbm.at[0], kv.at[own_rows, pl.ds(HEAD_DIM, HEAD_DIM)]),
        (b_hbm.at[0], b_ref),
        (x_hbm.at[0], x_ref),
        (own_hbm, own_ref),
        (c_hbm.at[0], c_ref),
        (skip_hbm, skip_ref),
        (z_hbm.at[0], z_ref),
        (gain_hbm, gain_ref),
    ] + [
        (
            q_hbm.at[0, :, pl.ds(a * HEAD_DIM, HEAD_DIM)],
            qa.at[pl.ds(a * rows, rows), pl.ds(0, HEAD_DIM)],
        )
        for a in range(q_heads)
    ]
    loads = [pltpu.make_async_copy(s, d, sem_in.at[i]) for i, (s, d) in enumerate(pairs)]
    for load in loads:
        load.start()

    barrier = pltpu.get_barrier_semaphore()

    for k in range(1, n):
        pl.semaphore_signal(
            barrier, inc=1, device_id={"seq": lax.rem(me + k, n)}, device_id_type=MESH
        )
    for k in range(1, n_pool):
        pl.semaphore_signal(
            barrier, inc=1, device_id={"pool": lax.rem(my_pool + k, n_pool)}, device_id_type=MESH
        )

    row_i = lax.broadcasted_iota(jnp.int32, (rows, rows), 0)
    col_i = lax.broadcasted_iota(jnp.int32, (rows, rows), 1)
    lower = (col_i <= row_i).astype(F32)
    unit = (col_i == row_i).astype(F32)
    head_of = lax.broadcasted_iota(jnp.int32, (heads, chans), 1) // HEAD_P
    grid = (head_of == lax.broadcasted_iota(jnp.int32, (heads, chans), 0)).astype(BF16)
    grid_two = jnp.concatenate([grid, grid], axis=0)
    for load in loads[:2]:
        load.wait()
    ld = ld_ref[...]
    cs = mm(ld, lower, NT, HIGH)
    cs_t = mm(lower, ld, NT, HIGH)
    seg_row = seg_ref[...].astype(F32)
    seg_rows = jnp.broadcast_to(seg_row, (8, rows))
    seg_col = mm(unit, seg_rows, NT)[:, 0:1]
    last_seg = seg_row[:, rows - 1 : rows]

    head_lane = jnp.concatenate(
        [jnp.exp(cs_t[rows - 1 : rows, :]), jnp.zeros((1, 128 - heads), F32)], axis=1
    )
    count_0 = jnp.sum(jnp.where(seg_row == 0.0, 1.0, 0.0), axis=1, keepdims=True)
    count_1 = jnp.sum(jnp.where(seg_row == 1.0, 1.0, 0.0), axis=1, keepdims=True)
    info = [head_lane] + [jnp.broadcast_to(v, (1, 128)) for v in (last_seg, count_0, count_1)]
    brief[half, mine_o] = jnp.concatenate(info + [jnp.zeros((4, 128), F32)], axis=0)

    pl.semaphore_wait(barrier, n - 1 + n_pool - 1)

    def peer(o):
        return (o // inner_n) * side + half * inner_n + lax.rem(o, inner_n)

    across = grp * side + (1 - half) * inner_n + lax.rem(place, inner_n)

    peers = []
    for i in range(1, owners_n):
        o = lax.rem(mine_o + i, owners_n)
        peers.append((o, peer(o)))

    def each_peer(act):
        for p in peers:
            act(p)

    def own_copy(k, p):
        return remote(
            send1.at[k, p[0]], recv1.at[k, mine_o], sem_1.at[0, k], sem_1.at[1, k], "seq", p[1]
        )

    def own_all(k):
        all_of = (k, pl.ds(0, owners_n - 1))
        return remote(
            send1.at[all_of], recv1.at[all_of], sem_1.at[0, k], sem_1.at[1, k], "seq", across
        )

    def brief_copy(p):
        at = brief.at[half, mine_o]
        return remote(at, at, sem_b.at[0, 0], sem_b.at[1, 0], "seq", p[1])

    def brief_all():
        at = brief.at[half, pl.ds(0, owners_n - 1)]
        return remote(at, at, sem_b.at[0, 0], sem_b.at[1, 0], "seq", across)

    def brief_across():
        at = brief.at[half]
        return remote(at, at, sem_b.at[0, 1], sem_b.at[1, 1], "seq", across)

    def kz_at(tract):
        at = pl.ds(pl.multiple_of(tract * rows, rows), rows)
        return kv.at[at]

    def kz_near(i, tract, which):
        to = grp * side + half * inner_n + lax.rem(lax.rem(place, inner_n) + i, inner_n)
        at = kz_at(tract)
        return remote(at, at, sem_kz.at[0, which], sem_kz.at[1, which], "seq", to)

    def kz_near_all(which):
        at = kv.at[pl.ds(0, (inner_n - 1) * rows)]
        return remote(at, at, sem_kz.at[0, which], sem_kz.at[1, which], "seq", across)

    def kz_far(tract):
        at = kz_at(tract)
        return remote(at, at, sem_kz.at[0, 1], sem_kz.at[1, 1], "seq", across)

    for load in loads[2:4]:
        load.wait()
    kz_far(me).start()
    for i in range(1, inner_n):
        kz_near(i, me, 0).start()
    each_peer(lambda p: brief_copy(p).start())

    tail_w = jnp.where(seg_col == last_seg, jnp.exp(cs_t[rows - 1 : rows, :] - cs_t), 0.0)
    tail_two = split_two(tail_w)
    for load in loads[4:6]:
        load.wait()
    b_t = b_ref[...].astype(F32).T.astype(BF16)
    for at in range(0, chans, 256):
        lanes = slice(at, at + 256)
        tail_x = (x_ref[:, lanes].astype(F32) * mm(tail_two, grid_two[:, lanes])).astype(BF16)
        state = mm(b_t, tail_x).astype(BF16)
        w, off = divmod(at, half_chans)
        for s in range(n):
            send1[(s % 2) * 2 + w, s // 2, :, off : off + 256] = state[s * n_rows : (s + 1) * n_rows]

    brief_all().wait_recv()
    brief_across().start()
    each_peer(lambda p: own_copy(0, p).start())
    for k in range(1, chunks):
        each_peer(lambda p: own_copy(k, p).start())
    for k in range(chunks):
        recv1[k, mine_o] = send1[k, mine_o]
    near = [brief[half, o] for o in range(owners_n)]
    links = []
    for g in range(groups):
        for i in range(1, inner_n):
            a, b = near[g * inner_n + i - 1], near[g * inner_n + i]
            links.append(jnp.where(a[1:2] == b[1:2], b[0:1], 0.0))
    if links:
        links = jnp.concatenate(links + [jnp.zeros((8 - len(links), 128), F32)], axis=0)
        links = expand(links[:, 0:heads], grid)
    kz_far(me).wait_recv()
    for i in range(1, inner_n):
        kz_near(i, across, 2).start()

    def sum_copy(k):
        return remote(
            sums.at[k],
            others.at[k, pl.ds(1, groups)],
            sem_p.at[0, k],
            sem_p.at[1, k],
            "seq",
            across,
        )

    def own_lanes(k):
        return slice((k % 2) * half_chans, (k % 2 + 1) * half_chans)

    def kx_copy(to_grp, src_grp):
        at = pl.ds(pl.multiple_of(src_grp * span, span), span)
        to = to_grp * side + place
        return remote(
            kv.at[at], kv.at[at], sem_kx.at[0, to_grp], sem_kx.at[1, src_grp], "seq", to
        )

    def kx_start():
        if inner_n > 1:
            kz_near_all(0).wait_recv()
            kz_near_all(2).wait_recv()
        for g in range(1, groups):

            @pl.when(grp < g)
            def _():
                kx_copy(g, grp).start()

    for k in range(chunks):
        if k == 0:
            kx_start()
        own_all(k).wait_recv()
        for g in range(groups):
            total = recv1[k, g * inner_n].astype(F32)
            for i in range(1, inner_n):
                at = g * (inner_n - 1) + i - 1
                keep = links[at : at + 1, own_lanes(k)]
                total = total * keep + recv1[k, g * inner_n + i].astype(F32)
            sums[k, g] = total.astype(BF16)
        sum_copy(k).start()

    loads[6].wait()
    owners = own_ref[...]
    for w in range(2):
        for o in range(n_pool):
            page = jnp.zeros((page_rows, HEAD_DIM), F32)
            for g in range(n_pool):
                at = pl.ds(pl.multiple_of(mine + g * page_rows, 16), page_rows)
                part = kv[at, w * HEAD_DIM : (w + 1) * HEAD_DIM].astype(F32)
                page = jnp.where(owners[:, g : g + 1] == o, part, page)
            pages[o, w] = page.astype(BF16)

    def page_copy(k, w):
        to = lax.rem(my_pool + k, n_pool)
        dst = (ok_out, ov_out)[w].at[0, my_pool]
        return remote(pages.at[to, w], dst, sem_pool.at[0, 0], sem_pool.at[1, 0], "pool", to)

    def page_all():
        at = pages.at[pl.ds(0, n_pool - 1)]
        to = lax.rem(my_pool + 1, n_pool)
        return remote(at, at, sem_pool.at[0, 0], sem_pool.at[1, 0], "pool", to)

    def last_copy(k):
        to = lax.rem(my_pool + k, n_pool)
        return remote(
            st_send.at[to], st_out.at[my_pool], sem_pool.at[0, 1], sem_pool.at[1, 1], "pool", to
        )

    def last_all():
        at = pl.ds(0, n_pool - 1)
        to = lax.rem(my_pool + 1, n_pool)
        return remote(
            st_send.at[at], st_out.at[at], sem_pool.at[0, 1], sem_pool.at[1, 1], "pool", to
        )

    for k in range(1, n_pool):
        for w in range(2):
            page_copy(k, w).start()
    stores = [
        pltpu.make_async_copy(pages.at[my_pool, 0], ok_out.at[0, my_pool], sem_out.at[0]),
        pltpu.make_async_copy(pages.at[my_pool, 1], ov_out.at[0, my_pool], sem_out.at[1]),
        pltpu.make_async_copy(st_send.at[my_pool], st_out.at[my_pool], sem_out.at[2]),
        pltpu.make_async_copy(att_v, att_out.at[0], sem_out.at[3]),
    ]
    stores[0].start()
    stores[1].start()

    brief_across().wait_recv()
    order = [
        brief[(c % side) // inner_n, (c // side) * inner_n + c % inner_n] for c in range(n)
    ]
    line = []
    for c in range(n):
        last = order[c][1:2]
        before = order[c - 1][1:2] if c else jnp.full((1, 128), -1.0, F32)
        line.append(jnp.where(last == before, order[c][0:1], 0.0))
    run = [
        [math.prod(line[g * side + h * inner_n + i] for i in range(inner_n)) for g in range(groups)]
        for h in range(2)
    ]
    table = [jnp.where(half == 0, run[1][max(g - 1, 0)], run[0][g]) for g in range(groups)]
    for g in range(groups):
        for i in range(inner_n):
            a, b = line[g * side + i], line[g * side + inner_n + i]
            table.append(jnp.where(half == 0, a, b))
    table.append(run[1][groups - 1])
    end_at = len(table) - 1
    table = jnp.concatenate(table + [jnp.zeros((16 - len(table), 128), F32)], axis=0)
    factor[...] = expand(table[:, 0:heads], grid)

    others[:, 0] = jnp.zeros_like(others[:, 0])

    def back_copy(k, p):
        return remote(
            send2.at[k, p[0]], recv2.at[k, mine_o], sem_2.at[0, k], sem_2.at[1, k], "seq", p[1]
        )

    def back_all(k):
        all_of = (k, pl.ds(0, owners_n - 1))
        return remote(
            send2.at[all_of], recv2.at[all_of], sem_2.at[0, k], sem_2.at[1, k], "seq", across
        )

    def fin_copy(k, p):
        return remote(
            fin_send.at[k, p[0]], fin_recv.at[k, mine_o], sem_f.at[0, k], sem_f.at[1, k], "seq", p[1]
        )

    def fin_all(k):
        at = (k, pl.ds(0, owners_n - 1))
        return remote(
            fin_send.at[at], fin_recv.at[at], sem_f.at[0, k], sem_f.at[1, k], "seq", across
        )

    def scan(k):
        lanes = own_lanes(k)
        sum_copy(k).wait_recv()
        carry = jnp.zeros((n_rows, half_chans), F32)
        for g in range(groups):
            carry = carry * factor[g : g + 1, lanes] + others[k, g + half].astype(F32)
            for i in range(inner_n):
                o = g * inner_n + i
                send2[k, o] = carry.astype(BF16)
                at = groups + o
                carry = carry * factor[at : at + 1, lanes] + recv1[k, o].astype(F32)
        each_peer(lambda p: back_copy(k, p).start())
        recv2[k, mine_o] = send2[k, mine_o]

        end = carry * factor[end_at : end_at + 1, lanes] + others[k, groups].astype(F32)
        last = jnp.where(half == 0, end, carry)
        count = tiles // 2
        stacked = jnp.concatenate([last[:, t * 128 : (t + 1) * 128] for t in range(count)], axis=0)
        fin_t[...] = stacked.T
        to_lanes = slice((k % 2) * count * n_rows, (k % 2 + 1) * count * n_rows)
        for o in range(owners_n):
            first = (o // inner_n) * side + o % inner_n
            for w in range(2):
                a = w * HEAD_P + first * p_rows
                b = a + inner_n * p_rows
                part = jnp.where(half == 0, fin_t[a : a + p_rows, :], fin_t[b : b + p_rows, :])
                fin_send[k // 2, o, w * p_rows : (w + 1) * p_rows, to_lanes] = part
        if k % 2:
            each_peer(lambda p: fin_copy(k // 2, p).start())
            fin_recv[k // 2, mine_o] = fin_send[k // 2, mine_o]

    scan(0)

    for load in loads[7:]:
        load.wait()
    edge_0 = sum(o[2:3] for o in order)
    edge_1 = edge_0 + sum(o[3:4] for o in order)
    prev = jnp.maximum(me - 1, 0)
    prev_o = (prev // side) * inner_n + lax.rem(prev, inner_n)
    prev_last = brief[lax.rem(prev, side) // inner_n, prev_o][1:2, 0:1]
    prev_last = jnp.where(me == 0, -1.0, prev_last)
    enter_two = split_two(jnp.where(seg_col == prev_last, jnp.exp(cs_t), 0.0))
    skip_x = expand(jnp.broadcast_to(skip_ref[...], (8, heads)), grid)[0:1]
    inner = mm(c_ref[...], b_t)
    inner = jnp.where((col_i <= row_i) & (seg_col == seg_row), inner, 0.0)
    first_half = lax.broadcasted_iota(jnp.int32, (rows, 128), 1) < HEAD_P

    def within(pair):
        lanes = slice(pair * 128, pair * 128 + 128)
        x_pair = x_ref[:, lanes]
        y = []
        for h in (2 * pair, 2 * pair + 1):
            gap = jnp.minimum(cs_t[:, h : h + 1] - cs[h : h + 1, :], 0.0)
            y.append(mm((inner * jnp.exp(gap)).astype(BF16), x_pair))
        mix0[:, lanes] = jnp.where(first_half, y[0], y[1]) + skip_x[:, lanes] * x_pair.astype(F32)
        gate = z_ref[:, lanes].astype(F32)
        silu_z[:, lanes] = gate / (1.0 + jnp.exp(-gate))
        enter_x[:, lanes] = mm(enter_two, grid_two[:, lanes])

    for pair in range(heads // 2):
        within(pair)

    scan(1)

    lane = lax.broadcasted_iota(jnp.int32, (rows, HEAD_DIM), 1).astype(F32)
    q_doc = jnp.where(lane == seg_col, 1.0, 0.0).astype(BF16)
    for a in range(q_heads):
        qa[a * rows : (a + 1) * rows, HEAD_DIM : 2 * HEAD_DIM] = q_doc

    scale = HEAD_DIM ** (-0.5) * LOG2E
    key_lane = lax.broadcasted_iota(jnp.int32, (HEAD_DIM, span), 1)
    doc_row = lax.broadcasted_iota(jnp.int32, (HEAD_DIM, span), 0)
    causal_key = lax.broadcasted_iota(jnp.int32, (rows, span), 1)
    causal_row = lax.broadcasted_iota(jnp.int32, (rows, span), 0)
    edges = [jnp.concatenate([e] * (span // 128), axis=1) for e in (edge_0, edge_1)]

    def attend(g, first):
        at = pl.ds(pl.multiple_of(g * span, span), span)
        key_pos = (key_lane + g * span).astype(F32)
        doc = jnp.where(key_pos >= edges[0], 1, 0) + jnp.where(key_pos >= edges[1], 1, 0)
        k_doc = jnp.where((doc != doc_row) & (doc_row < 3), FAR, 0.0).astype(BF16)
        k_t = kv[at, 0:HEAD_DIM].astype(F32).T.astype(BF16)
        keys = jnp.concatenate([k_t, k_doc], axis=0)
        for a in range(q_heads):
            own = slice(a * rows, (a + 1) * rows)
            s = mm(qa[own, :], keys)
            if first:
                s = jnp.where(causal_key + g * span <= causal_row + me * rows, s, FAR)
            score[own, :] = s
            top = functools.reduce(jnp.maximum, [s[:, i : i + 128] for i in range(0, span, 128)])
            if not first:
                top = jnp.maximum(top, run_max[own])
            top = jnp.broadcast_to(jnp.max(top, axis=1, keepdims=True), (rows, 128))
            if not first:
                shrink = jnp.exp2((run_max[own] - top) * scale)
                run_sum[own] = run_sum[own] * shrink
                run_out[own] = run_out[own] * shrink
            run_max[own] = top
        values = kv[at, HEAD_DIM : 2 * HEAD_DIM]
        for a in range(q_heads):
            own = slice(a * rows, (a + 1) * rows)
            top = run_max[own]
            total = None if first else run_sum[own]
            weights = []
            for i in range(0, span, 128):
                e = jnp.exp2((score[own, i : i + 128] - top) * scale)
                total = e if total is None else total + e
                weights.append(e.astype(BF16))
            out = mm(jnp.concatenate(weights, axis=1), values)
            run_sum[own] = total
            run_out[own] = out if first else run_out[own] + out

    attend(grp, True)

    def attend_earlier(g):
        kx_copy(g, g).wait_recv()
        attend(g, False)

    def attend_rest(i, u):
        attend_earlier(grp - 1 - i)
        return u

    scan(2)
    scan(3)
    lax.fori_loop(0, grp, attend_rest, 0)
    for a in range(q_heads):
        own = slice(a * rows, (a + 1) * rows)
        total = jnp.sum(run_sum[own], axis=1, keepdims=True)
        att_v[:, a * HEAD_DIM : (a + 1) * HEAD_DIM] = (run_out[own] / total).astype(BF16)
    stores[3].start()


    for k in range(2):
        fin_all(k).wait_recv()
    last = [
        jnp.concatenate(
            [fin_recv[s % 2, s // 2, :, t * n_rows : (t + 1) * n_rows] for s in range(n)], axis=1
        )
        for t in range(tiles)
    ]
    per = tiles // n_pool
    for o in range(n_pool):
        for t in range(per):
            part = jnp.zeros_like(last[0])
            for g in range(n_pool):
                part = jnp.where(owners[:, g : g + 1] == o, last[g * per + t], part)
            for w in range(2):
                st_send[o, 2 * t + w] = part[w * p_rows : (w + 1) * p_rows]
    for k in range(1, n_pool):
        last_copy(k).start()
    stores[2].start()

    for k in range(chunks):
        own_all(k).wait_send()
        sum_copy(k).wait_send()
        back_all(k).wait_send()
    brief_all().wait_send()
    brief_across().wait_send()
    for k in range(2):
        fin_all(k).wait_send()
    kz_far(me).wait_send()
    if inner_n > 1:
        kz_near_all(0).wait_send()
        kz_near_all(2).wait_send()
    for g in range(1, groups):

        @pl.when(grp < g)
        def _():
            kx_copy(g, grp).wait_send()

    if n_pool > 1:
        page_all().wait()

    for k in range(chunks):
        back_all(k).wait_recv()
    c_all = c_ref[...]
    square = jnp.zeros((rows, 128), F32)
    for at in range(0, chans, 256):
        lanes = slice(at, at + 256)
        w, off = divmod(at, half_chans)
        entered = jnp.concatenate(
            [recv2[(s % 2) * 2 + w, s // 2, :, off : off + 256] for s in range(n)], axis=0
        )
        y = mm(c_all, entered)
        mixed = (mix0[:, lanes] + y * enter_x[:, lanes]).astype(BF16).astype(F32)
        gated = mixed * silu_z[:, lanes]
        mix0[:, lanes] = gated
        square = square + gated[:, 0:128] * gated[:, 0:128] + gated[:, 128:] * gated[:, 128:]
    mean = jnp.sum(square, axis=1, keepdims=True) * (1.0 / chans)
    norm = lax.rsqrt(mean + NORM_EPS)
    part = chans // 4
    for at in range(0, chans, 256):
        lanes = slice(at, at + 256)
        mix_v[:, lanes] = (mix0[:, lanes] * norm * gain_ref[:, lanes]).astype(BF16)
        if (at + 256) % part == 0:
            done = pl.ds(at + 256 - part, part)
            store = pltpu.make_async_copy(
                mix_v.at[:, done], mix_out.at[0, :, done], sem_out.at[4 + at // part]
            )
            store.start()
            stores.append(store)
    if n_pool > 1:
        last_all().wait()
    for store in stores:
        store.wait()


def store(*refs):
    count = (len(refs) - 2) // 3
    sem_in, sem_out = refs[-2:]
    through = refs[2 * count : 3 * count]
    loads = [pltpu.make_async_copy(refs[i], through[i], sem_in.at[i]) for i in range(count)]
    saves = [
        pltpu.make_async_copy(through[i], refs[count + i], sem_out.at[i]) for i in range(count)
    ]
    for load in loads:
        load.start()
    for load, save in zip(loads, saves):
        load.wait()
        save.start()
    for save in saves:
        save.wait()


def local(n, n_pool, *args):
    (x, z, b, c, ld, skip, gain, seg, q, k, v, owner) = args
    rows, chans = x.shape[1:]
    heads = ld.shape[1]
    q_heads = q.shape[2] // HEAD_DIM
    p_rows = HEAD_P // n
    n_rows = STATE // n
    side = math.isqrt(n)
    groups = n // side
    owners_n = n // 2
    grp_heads = heads // n_pool
    page_rows = rows // n_pool
    tiles = chans // 128
    hbm = pl.BlockSpec(memory_space=pltpu.HBM)
    pages = (n_pool, page_rows, HEAD_DIM)
    states = (n_pool, grp_heads, p_rows, STATE)
    part = (4, owners_n, n_rows, chans // 2)
    dma = pltpu.SemaphoreType.DMA
    out = pl.pallas_call(
        functools.partial(kernel, n, n_pool),
        out_shape=(
            jax.ShapeDtypeStruct(x.shape, BF16),
            jax.ShapeDtypeStruct(q.shape, BF16),
            jax.ShapeDtypeStruct(states, F32),
            jax.ShapeDtypeStruct((1,) + pages, BF16),
            jax.ShapeDtypeStruct((1,) + pages, BF16),
        ),
        in_specs=[hbm] * 12,
        out_specs=[hbm] * 5,
        scratch_shapes=[
            pltpu.VMEM((rows, chans), BF16),
            pltpu.VMEM((rows, q_heads * HEAD_DIM), BF16),
            pltpu.VMEM((rows, chans), BF16),
            pltpu.VMEM((rows, chans), BF16),
            pltpu.VMEM((rows, STATE), BF16),
            pltpu.VMEM((rows, STATE), BF16),
            pltpu.VMEM((heads, rows), F32),
            pltpu.VMEM((1, heads), F32),
            pltpu.VMEM((1, chans), F32),
            pltpu.VMEM((1, rows), jnp.int32),
            pltpu.VMEM(owner.shape, jnp.int32),
            pltpu.VMEM((q_heads * rows, 2 * HEAD_DIM), BF16),
            pltpu.VMEM((n * rows, 2 * HEAD_DIM), BF16),
            pltpu.VMEM(part, BF16),
            pltpu.VMEM(part, BF16),
            pltpu.VMEM((4, groups, n_rows, chans // 2), BF16),
            pltpu.VMEM((4, groups + 1, n_rows, chans // 2), BF16),
            pltpu.VMEM(part, BF16),
            pltpu.VMEM(part, BF16),
            pltpu.VMEM((2, owners_n, 8, 128), F32),
            pltpu.VMEM((16, chans), F32),
            pltpu.VMEM((q_heads * rows, side * rows), F32),
            pltpu.VMEM((q_heads * rows, 128), F32),
            pltpu.VMEM((q_heads * rows, 128), F32),
            pltpu.VMEM((q_heads * rows, HEAD_DIM), F32),
            pltpu.VMEM((rows, chans), F32),
            pltpu.VMEM((rows, chans), F32),
            pltpu.VMEM((rows, chans), F32),
            pltpu.VMEM((n_pool, 2, page_rows, HEAD_DIM), BF16),
            pltpu.VMEM((128, tiles // 2 * n_rows), F32),
            pltpu.VMEM((2, owners_n, 2 * p_rows, tiles * n_rows), F32),
            pltpu.VMEM((2, owners_n, 2 * p_rows, tiles * n_rows), F32),
            pltpu.VMEM(states, F32),
            dma((11 + q_heads,)),
            dma((8,)),
            dma((2, 2)),
            dma((2, 4)),
            dma((2, 4)),
            dma((2, 4)),
            dma((2, 2)),
            dma((2, 3)),
            dma((2, 4)),
            dma((2, 2)),
        ],
        compiler_params=pltpu.CompilerParams(
            collective_id=0, has_side_effects=True, vmem_limit_bytes=60 * 1024 * 1024
        ),
    )(x, z, b, c, ld, skip.reshape(1, -1), gain.reshape(1, -1), seg, q, k, v, owner)
    out = pl.pallas_call(
        store,
        out_shape=tuple(jax.ShapeDtypeStruct(o.shape, o.dtype) for o in out),
        in_specs=[hbm] * 5,
        out_specs=[hbm] * 5,
        scratch_shapes=[pltpu.VMEM(o.shape, o.dtype) for o in out] + [dma((5,)), dma((5,))],
        compiler_params=pltpu.CompilerParams(vmem_limit_bytes=60 * 1024 * 1024),
    )(*out)
    mixer, attended, owned, keys, values = out
    return mixer, attended, owned[None], keys, values


def solution(mesh):
    return jax.shard_map(
        functools.partial(local, mesh.shape["seq"], mesh.shape["pool"]),
        mesh=mesh,
        in_specs=(
            P("pool", "seq", "head"),
            P("pool", "seq", "head"),
            P("pool", "seq", "head"),
            P("pool", "seq", "head"),
            P("pool", "head", "seq"),
            P("head"),
            P("head"),
            P("pool", "seq"),
            P("pool", "seq", "head"),
            P("pool", "seq", "head"),
            P("pool", "seq", "head"),
            P("pool", "head"),
        ),
        out_specs=(
            P("pool", "seq", "head"),
            P("pool", "seq", "head"),
            P("pool", None, "head", "seq", None),
            P("pool", None, "seq", "head"),
            P("pool", None, "seq", "head"),
        ),
        check_vma=False,
    )
```

```python
import functools
import math

import jax
import jax.numpy as jnp
from jax import lax
from jax.experimental import pallas as pl
from jax.experimental.pallas import tpu as pltpu
from jax.sharding import PartitionSpec as P

HEAD_P = 64
STATE = 256
HEAD_DIM = 128
NORM_EPS = 1e-05
HIGH = lax.Precision.HIGHEST
LOG2E = math.log2(math.e)
FAR = -1e30
F32 = jnp.float32
BF16 = jnp.bfloat16
MESH = pl.DeviceIdType.MESH
NN = (((1,), (0,)), ((), ()))
NT = (((1,), (1,)), ((), ()))


def mm(a, b, dims=NN, precision=None):
    return lax.dot_general(a, b, dims, precision=precision, preferred_element_type=F32)


def expand(parts, grid):
    high = parts.astype(BF16)
    rest = parts - high.astype(F32)
    middle = rest.astype(BF16)
    low = (rest - middle.astype(F32)).astype(BF16)
    return mm(high, grid) + mm(middle, grid) + mm(low, grid)


def split_two(parts):
    high = parts.astype(BF16)
    return jnp.concatenate([high, (parts - high.astype(F32)).astype(BF16)], axis=1)


def kernel(
    n,
    n_pool,
    x_hbm,
    z_hbm,
    b_hbm,
    c_hbm,
    ld_hbm,
    skip_hbm,
    gain_hbm,
    seg_hbm,
    q_hbm,
    k_hbm,
    v_hbm,
    own_hbm,
    mix_out,
    att_out,
    st_out,
    ok_out,
    ov_out,
    mix_v,
    att_v,
    x_ref,
    z_ref,
    b_ref,
    c_ref,
    ld_ref,
    skip_ref,
    gain_ref,
    seg_ref,
    own_ref,
    qa,
    kv,
    send1,
    recv1,
    sums,
    others,
    send2,
    recv2,
    brief,
    factor,
    score,
    run_max,
    run_sum,
    run_out,
    mix0,
    enter_x,
    silu_z,
    pages,
    fin_t,
    fin_send,
    fin_recv,
    st_send,
    sem_in,
    sem_out,
    sem_b,
    sem_1,
    sem_p,
    sem_2,
    sem_f,
    sem_kz,
    sem_kx,
    sem_pool,
):
    rows = x_hbm.shape[1]
    chans = x_hbm.shape[2]
    heads = ld_hbm.shape[1]
    q_heads = q_hbm.shape[2] // HEAD_DIM
    p_rows = HEAD_P // n
    n_rows = STATE // n
    side = math.isqrt(n)
    groups = n // side
    inner_n = side // 2
    owners_n = groups * inner_n
    half_chans = chans // 2
    chunks = 4
    span = side * rows
    page_rows = rows // n_pool
    grp_heads = heads // n_pool
    tiles = chans // 128
    me = lax.axis_index("seq")
    my_pool = lax.axis_index("pool")
    grp = me // side
    place = lax.rem(me, side)
    half = place // inner_n
    mine_o = grp * inner_n + lax.rem(place, inner_n)
    mine = pl.multiple_of(me * rows, rows)

    def remote(src, dst, send_sem, recv_sem, axis, to):
        return pltpu.make_async_remote_copy(
            src_ref=src,
            dst_ref=dst,
            send_sem=send_sem,
            recv_sem=recv_sem,
            device_id={axis: to},
            device_id_type=MESH,
        )

    own_rows = pl.ds(mine, rows)
    pairs = [
        (ld_hbm.at[0], ld_ref),
        (seg_hbm, seg_ref),
        (k_hbm.at[0], kv.at[own_rows, pl.ds(0, HEAD_DIM)]),
        (v_hbm.at[0], kv.at[own_rows, pl.ds(HEAD_DIM, HEAD_DIM)]),
        (b_hbm.at[0], b_ref),
        (x_hbm.at[0], x_ref),
        (own_hbm, own_ref),
        (c_hbm.at[0], c_ref),
        (skip_hbm, skip_ref),
        (z_hbm.at[0], z_ref),
        (gain_hbm, gain_ref),
    ] + [
        (
            q_hbm.at[0, :, pl.ds(a * HEAD_DIM, HEAD_DIM)],
            qa.at[pl.ds(a * rows, rows), pl.ds(0, HEAD_DIM)],
        )
        for a in range(q_heads)
    ]
    loads = [pltpu.make_async_copy(s, d, sem_in.at[i]) for i, (s, d) in enumerate(pairs)]
    for load in loads:
        load.start()

    barrier = pltpu.get_barrier_semaphore()

    for k in range(1, n):
        pl.semaphore_signal(
            barrier, inc=1, device_id={"seq": lax.rem(me + k, n)}, device_id_type=MESH
        )
    for k in range(1, n_pool):
        pl.semaphore_signal(
            barrier, inc=1, device_id={"pool": lax.rem(my_pool + k, n_pool)}, device_id_type=MESH
        )

    row_i = lax.broadcasted_iota(jnp.int32, (rows, rows), 0)
    col_i = lax.broadcasted_iota(jnp.int32, (rows, rows), 1)
    lower = (col_i <= row_i).astype(F32)
    unit = (col_i == row_i).astype(F32)
    head_of = lax.broadcasted_iota(jnp.int32, (heads, chans), 1) // HEAD_P
    grid = (head_of == lax.broadcasted_iota(jnp.int32, (heads, chans), 0)).astype(BF16)
    grid_two = jnp.concatenate([grid, grid], axis=0)
    for load in loads[:2]:
        load.wait()
    ld = ld_ref[...]
    cs = mm(ld, lower, NT, HIGH)
    cs_t = mm(lower, ld, NT, HIGH)
    seg_row = seg_ref[...].astype(F32)
    seg_rows = jnp.broadcast_to(seg_row, (8, rows))
    seg_col = mm(unit, seg_rows, NT)[:, 0:1]
    last_seg = seg_row[:, rows - 1 : rows]

    head_lane = jnp.concatenate(
        [jnp.exp(cs_t[rows - 1 : rows, :]), jnp.zeros((1, 128 - heads), F32)], axis=1
    )
    count_0 = jnp.sum(jnp.where(seg_row == 0.0, 1.0, 0.0), axis=1, keepdims=True)
    count_1 = jnp.sum(jnp.where(seg_row == 1.0, 1.0, 0.0), axis=1, keepdims=True)
    info = [head_lane] + [jnp.broadcast_to(v, (1, 128)) for v in (last_seg, count_0, count_1)]
    brief[half, mine_o] = jnp.concatenate(info + [jnp.zeros((4, 128), F32)], axis=0)

    pl.semaphore_wait(barrier, n - 1 + n_pool - 1)

    def peer(o):
        return (o // inner_n) * side + half * inner_n + lax.rem(o, inner_n)

    across = grp * side + (1 - half) * inner_n + lax.rem(place, inner_n)

    peers = []
    for i in range(1, owners_n):
        o = lax.rem(mine_o + i, owners_n)
        peers.append((o, peer(o)))

    def each_peer(act):
        for p in peers:
            act(p)

    def own_copy(k, p):
        return remote(
            send1.at[k, p[0]], recv1.at[k, mine_o], sem_1.at[0, k], sem_1.at[1, k], "seq", p[1]
        )

    def own_all(k):
        all_of = (k, pl.ds(0, owners_n - 1))
        return remote(
            send1.at[all_of], recv1.at[all_of], sem_1.at[0, k], sem_1.at[1, k], "seq", across
        )

    def brief_copy(p):
        at = brief.at[half, mine_o]
        return remote(at, at, sem_b.at[0, 0], sem_b.at[1, 0], "seq", p[1])

    def brief_all():
        at = brief.at[half, pl.ds(0, owners_n - 1)]
        return remote(at, at, sem_b.at[0, 0], sem_b.at[1, 0], "seq", across)

    def brief_across():
        at = brief.at[half]
        return remote(at, at, sem_b.at[0, 1], sem_b.at[1, 1], "seq", across)

    def kz_at(tract):
        at = pl.ds(pl.multiple_of(tract * rows, rows), rows)
        return kv.at[at]

    def kz_near(i, tract, which):
        to = grp * side + half * inner_n + lax.rem(lax.rem(place, inner_n) + i, inner_n)
        at = kz_at(tract)
        return remote(at, at, sem_kz.at[0, which], sem_kz.at[1, which], "seq", to)

    def kz_near_all(which):
        at = kv.at[pl.ds(0, (inner_n - 1) * rows)]
        return remote(at, at, sem_kz.at[0, which], sem_kz.at[1, which], "seq", across)

    def kz_far(tract):
        at = kz_at(tract)
        return remote(at, at, sem_kz.at[0, 1], sem_kz.at[1, 1], "seq", across)

    for load in loads[2:4]:
        load.wait()
    kz_far(me).start()
    for i in range(1, inner_n):
        kz_near(i, me, 0).start()
    each_peer(lambda p: brief_copy(p).start())

    tail_w = jnp.where(seg_col == last_seg, jnp.exp(cs_t[rows - 1 : rows, :] - cs_t), 0.0)
    tail_two = split_two(tail_w)
    for load in loads[4:6]:
        load.wait()
    b_t = b_ref[...].astype(F32).T.astype(BF16)
    def make_state(at):
        lanes = slice(at, at + 256)
        tail_x = (x_ref[:, lanes].astype(F32) * mm(tail_two, grid_two[:, lanes])).astype(BF16)
        state = mm(b_t, tail_x).astype(BF16)
        w, off = divmod(at, half_chans)
        for s in range(n):
            send1[(s % 2) * 2 + w, s // 2, :, off : off + 256] = state[s * n_rows : (s + 1) * n_rows]

    for at in range(0, half_chans, 256):
        make_state(at)
    brief_all().wait_recv()
    brief_across().start()
    each_peer(lambda p: own_copy(0, p).start())
    for at in range(half_chans, chans, 256):
        make_state(at)
    for k in range(1, chunks):
        each_peer(lambda p: own_copy(k, p).start())
    for k in range(chunks):
        recv1[k, mine_o] = send1[k, mine_o]
    near = [brief[half, o] for o in range(owners_n)]
    links = []
    for g in range(groups):
        for i in range(1, inner_n):
            a, b = near[g * inner_n + i - 1], near[g * inner_n + i]
            links.append(jnp.where(a[1:2] == b[1:2], b[0:1], 0.0))
    if links:
        links = jnp.concatenate(links + [jnp.zeros((8 - len(links), 128), F32)], axis=0)
        links = expand(links[:, 0:heads], grid)
    kz_far(me).wait_recv()
    for i in range(1, inner_n):
        kz_near(i, across, 2).start()

    def sum_copy(k):
        return remote(
            sums.at[k],
            others.at[k, pl.ds(1, groups)],
            sem_p.at[0, k],
            sem_p.at[1, k],
            "seq",
            across,
        )

    def own_lanes(k):
        return slice((k % 2) * half_chans, (k % 2 + 1) * half_chans)

    def kx_copy(to_grp, src_grp):
        at = pl.ds(pl.multiple_of(src_grp * span, span), span)
        to = to_grp * side + place
        return remote(
            kv.at[at], kv.at[at], sem_kx.at[0, to_grp], sem_kx.at[1, src_grp], "seq", to
        )

    def kx_start():
        if inner_n > 1:
            kz_near_all(0).wait_recv()
            kz_near_all(2).wait_recv()
        for g in range(1, groups):

            @pl.when(grp < g)
            def _():
                kx_copy(g, grp).start()

    for k in range(chunks):
        if k == 0:
            kx_start()
        own_all(k).wait_recv()
        for g in range(groups):
            total = recv1[k, g * inner_n].astype(F32)
            for i in range(1, inner_n):
                at = g * (inner_n - 1) + i - 1
                keep = links[at : at + 1, own_lanes(k)]
                total = total * keep + recv1[k, g * inner_n + i].astype(F32)
            sums[k, g] = total.astype(BF16)
        sum_copy(k).start()

    loads[6].wait()
    owners = own_ref[...]
    for w in range(2):
        for o in range(n_pool):
            page = jnp.zeros((page_rows, HEAD_DIM), F32)
            for g in range(n_pool):
                at = pl.ds(pl.multiple_of(mine + g * page_rows, 16), page_rows)
                part = kv[at, w * HEAD_DIM : (w + 1) * HEAD_DIM].astype(F32)
                page = jnp.where(owners[:, g : g + 1] == o, part, page)
            pages[o, w] = page.astype(BF16)

    def page_copy(k, w):
        to = lax.rem(my_pool + k, n_pool)
        dst = (ok_out, ov_out)[w].at[0, my_pool]
        return remote(pages.at[to, w], dst, sem_pool.at[0, 0], sem_pool.at[1, 0], "pool", to)

    def page_all():
        at = pages.at[pl.ds(0, n_pool - 1)]
        to = lax.rem(my_pool + 1, n_pool)
        return remote(at, at, sem_pool.at[0, 0], sem_pool.at[1, 0], "pool", to)

    def last_copy(k):
        to = lax.rem(my_pool + k, n_pool)
        return remote(
            st_send.at[to], st_out.at[my_pool], sem_pool.at[0, 1], sem_pool.at[1, 1], "pool", to
        )

    def last_all():
        at = pl.ds(0, n_pool - 1)
        to = lax.rem(my_pool + 1, n_pool)
        return remote(
            st_send.at[at], st_out.at[at], sem_pool.at[0, 1], sem_pool.at[1, 1], "pool", to
        )

    for k in range(1, n_pool):
        for w in range(2):
            page_copy(k, w).start()
    stores = [
        pltpu.make_async_copy(pages.at[my_pool, 0], ok_out.at[0, my_pool], sem_out.at[0]),
        pltpu.make_async_copy(pages.at[my_pool, 1], ov_out.at[0, my_pool], sem_out.at[1]),
        pltpu.make_async_copy(st_send.at[my_pool], st_out.at[my_pool], sem_out.at[2]),
        pltpu.make_async_copy(att_v, att_out.at[0], sem_out.at[3]),
    ]
    stores[0].start()
    stores[1].start()

    brief_across().wait_recv()
    order = [
        brief[(c % side) // inner_n, (c // side) * inner_n + c % inner_n] for c in range(n)
    ]
    line = []
    for c in range(n):
        last = order[c][1:2]
        before = order[c - 1][1:2] if c else jnp.full((1, 128), -1.0, F32)
        line.append(jnp.where(last == before, order[c][0:1], 0.0))
    run = [
        [math.prod(line[g * side + h * inner_n + i] for i in range(inner_n)) for g in range(groups)]
        for h in range(2)
    ]
    table = [jnp.where(half == 0, run[1][max(g - 1, 0)], run[0][g]) for g in range(groups)]
    for g in range(groups):
        for i in range(inner_n):
            a, b = line[g * side + i], line[g * side + inner_n + i]
            table.append(jnp.where(half == 0, a, b))
    table.append(run[1][groups - 1])
    end_at = len(table) - 1
    table = jnp.concatenate(table + [jnp.zeros((16 - len(table), 128), F32)], axis=0)
    factor[...] = expand(table[:, 0:heads], grid)

    others[:, 0] = jnp.zeros_like(others[:, 0])

    def back_copy(k, p):
        return remote(
            send2.at[k, p[0]], recv2.at[k, mine_o], sem_2.at[0, k], sem_2.at[1, k], "seq", p[1]
        )

    def back_all(k):
        all_of = (k, pl.ds(0, owners_n - 1))
        return remote(
            send2.at[all_of], recv2.at[all_of], sem_2.at[0, k], sem_2.at[1, k], "seq", across
        )

    def fin_copy(k, p):
        return remote(
            fin_send.at[k, p[0]], fin_recv.at[k, mine_o], sem_f.at[0, k], sem_f.at[1, k], "seq", p[1]
        )

    def fin_all(k):
        at = (k, pl.ds(0, owners_n - 1))
        return remote(
            fin_send.at[at], fin_recv.at[at], sem_f.at[0, k], sem_f.at[1, k], "seq", across
        )

    def scan(k):
        lanes = own_lanes(k)
        sum_copy(k).wait_recv()
        carry = jnp.zeros((n_rows, half_chans), F32)
        for g in range(groups):
            carry = carry * factor[g : g + 1, lanes] + others[k, g + half].astype(F32)
            for i in range(inner_n):
                o = g * inner_n + i
                send2[k, o] = carry.astype(BF16)
                at = groups + o
                carry = carry * factor[at : at + 1, lanes] + recv1[k, o].astype(F32)
        each_peer(lambda p: back_copy(k, p).start())
        recv2[k, mine_o] = send2[k, mine_o]

        end = carry * factor[end_at : end_at + 1, lanes] + others[k, groups].astype(F32)
        last = jnp.where(half == 0, end, carry)
        count = tiles // 2
        stacked = jnp.concatenate([last[:, t * 128 : (t + 1) * 128] for t in range(count)], axis=0)
        fin_t[...] = stacked.T
        to_lanes = slice((k % 2) * count * n_rows, (k % 2 + 1) * count * n_rows)
        for o in range(owners_n):
            first = (o // inner_n) * side + o % inner_n
            for w in range(2):
                a = w * HEAD_P + first * p_rows
                b = a + inner_n * p_rows
                part = jnp.where(half == 0, fin_t[a : a + p_rows, :], fin_t[b : b + p_rows, :])
                fin_send[k // 2, o, w * p_rows : (w + 1) * p_rows, to_lanes] = part
        if k % 2:
            each_peer(lambda p: fin_copy(k // 2, p).start())
            fin_recv[k // 2, mine_o] = fin_send[k // 2, mine_o]

    scan(0)

    for load in loads[7:]:
        load.wait()
    edge_0 = sum(o[2:3] for o in order)
    edge_1 = edge_0 + sum(o[3:4] for o in order)
    prev = jnp.maximum(me - 1, 0)
    prev_o = (prev // side) * inner_n + lax.rem(prev, inner_n)
    prev_last = brief[lax.rem(prev, side) // inner_n, prev_o][1:2, 0:1]
    prev_last = jnp.where(me == 0, -1.0, prev_last)
    enter_two = split_two(jnp.where(seg_col == prev_last, jnp.exp(cs_t), 0.0))
    skip_x = expand(jnp.broadcast_to(skip_ref[...], (8, heads)), grid)[0:1]
    inner = mm(c_ref[...], b_t)
    inner = jnp.where((col_i <= row_i) & (seg_col == seg_row), inner, 0.0)
    first_half = lax.broadcasted_iota(jnp.int32, (rows, 128), 1) < HEAD_P

    def within(pair):
        lanes = slice(pair * 128, pair * 128 + 128)
        x_pair = x_ref[:, lanes]
        y = []
        for h in (2 * pair, 2 * pair + 1):
            gap = jnp.minimum(cs_t[:, h : h + 1] - cs[h : h + 1, :], 0.0)
            y.append(mm((inner * jnp.exp(gap)).astype(BF16), x_pair))
        mix0[:, lanes] = jnp.where(first_half, y[0], y[1]) + skip_x[:, lanes] * x_pair.astype(F32)
        gate = z_ref[:, lanes].astype(F32)
        silu_z[:, lanes] = gate / (1.0 + jnp.exp(-gate))
        enter_x[:, lanes] = mm(enter_two, grid_two[:, lanes])

    for pair in range(heads // 2):
        within(pair)

    scan(1)

    lane = lax.broadcasted_iota(jnp.int32, (rows, HEAD_DIM), 1).astype(F32)
    q_doc = jnp.where(lane == seg_col, 1.0, 0.0).astype(BF16)
    for a in range(q_heads):
        qa[a * rows : (a + 1) * rows, HEAD_DIM : 2 * HEAD_DIM] = q_doc

    scale = HEAD_DIM ** (-0.5) * LOG2E
    key_lane = lax.broadcasted_iota(jnp.int32, (HEAD_DIM, span), 1)
    doc_row = lax.broadcasted_iota(jnp.int32, (HEAD_DIM, span), 0)
    causal_key = lax.broadcasted_iota(jnp.int32, (rows, span), 1)
    causal_row = lax.broadcasted_iota(jnp.int32, (rows, span), 0)
    edges = [jnp.concatenate([e] * (span // 128), axis=1) for e in (edge_0, edge_1)]

    def attend(g, first):
        at = pl.ds(pl.multiple_of(g * span, span), span)
        key_pos = (key_lane + g * span).astype(F32)
        doc = jnp.where(key_pos >= edges[0], 1, 0) + jnp.where(key_pos >= edges[1], 1, 0)
        k_doc = jnp.where((doc != doc_row) & (doc_row < 3), FAR, 0.0).astype(BF16)
        k_t = kv[at, 0:HEAD_DIM].astype(F32).T.astype(BF16)
        keys = jnp.concatenate([k_t, k_doc], axis=0)
        for a in range(q_heads):
            own = slice(a * rows, (a + 1) * rows)
            s = mm(qa[own, :], keys)
            if first:
                s = jnp.where(causal_key + g * span <= causal_row + me * rows, s, FAR)
            score[own, :] = s
            top = functools.reduce(jnp.maximum, [s[:, i : i + 128] for i in range(0, span, 128)])
            if not first:
                top = jnp.maximum(top, run_max[own])
            top = jnp.broadcast_to(jnp.max(top, axis=1, keepdims=True), (rows, 128))
            if not first:
                shrink = jnp.exp2((run_max[own] - top) * scale)
                run_sum[own] = run_sum[own] * shrink
                run_out[own] = run_out[own] * shrink
            run_max[own] = top
        values = kv[at, HEAD_DIM : 2 * HEAD_DIM]
        for a in range(q_heads):
            own = slice(a * rows, (a + 1) * rows)
            top = run_max[own]
            total = None if first else run_sum[own]
            weights = []
            for i in range(0, span, 128):
                e = jnp.exp2((score[own, i : i + 128] - top) * scale)
                total = e if total is None else total + e
                weights.append(e.astype(BF16))
            out = mm(jnp.concatenate(weights, axis=1), values)
            run_sum[own] = total
            run_out[own] = out if first else run_out[own] + out

    attend(grp, True)

    def attend_earlier(g):
        kx_copy(g, g).wait_recv()
        attend(g, False)

    def attend_rest(i, u):
        attend_earlier(grp - 1 - i)
        return u

    scan(2)
    scan(3)
    lax.fori_loop(0, grp, attend_rest, 0)
    for a in range(q_heads):
        own = slice(a * rows, (a + 1) * rows)
        total = jnp.sum(run_sum[own], axis=1, keepdims=True)
        att_v[:, a * HEAD_DIM : (a + 1) * HEAD_DIM] = (run_out[own] / total).astype(BF16)
    stores[3].start()


    for k in range(2):
        fin_all(k).wait_recv()
    last = [
        jnp.concatenate(
            [fin_recv[s % 2, s // 2, :, t * n_rows : (t + 1) * n_rows] for s in range(n)], axis=1
        )
        for t in range(tiles)
    ]
    per = tiles // n_pool
    for o in range(n_pool):
        for t in range(per):
            part = jnp.zeros_like(last[0])
            for g in range(n_pool):
                part = jnp.where(owners[:, g : g + 1] == o, last[g * per + t], part)
            for w in range(2):
                st_send[o, 2 * t + w] = part[w * p_rows : (w + 1) * p_rows]
    for k in range(1, n_pool):
        last_copy(k).start()
    stores[2].start()

    c_all = c_ref[...]
    square = jnp.zeros((rows, 128), F32)
    for at in range(0, chans, 256):
        lanes = slice(at, at + 256)
        w, off = divmod(at, half_chans)
        if off == 0:
            back_all(w).wait_recv()
            back_all(w + 2).wait_recv()
        entered = jnp.concatenate(
            [recv2[(s % 2) * 2 + w, s // 2, :, off : off + 256] for s in range(n)], axis=0
        )
        y = mm(c_all, entered)
        mixed = (mix0[:, lanes] + y * enter_x[:, lanes]).astype(BF16).astype(F32)
        gated = mixed * silu_z[:, lanes]
        mix0[:, lanes] = gated
        square = square + gated[:, 0:128] * gated[:, 0:128] + gated[:, 128:] * gated[:, 128:]
    mean = jnp.sum(square, axis=1, keepdims=True) * (1.0 / chans)
    norm = lax.rsqrt(mean + NORM_EPS)
    part = chans // 4
    for at in range(0, chans, 256):
        lanes = slice(at, at + 256)
        mix_v[:, lanes] = (mix0[:, lanes] * norm * gain_ref[:, lanes]).astype(BF16)
        if (at + 256) % part == 0:
            done = pl.ds(at + 256 - part, part)
            store = pltpu.make_async_copy(
                mix_v.at[:, done], mix_out.at[0, :, done], sem_out.at[4 + at // part]
            )
            store.start()
            stores.append(store)
    for k in range(chunks):
        own_all(k).wait_send()
        sum_copy(k).wait_send()
        back_all(k).wait_send()
    brief_all().wait_send()
    brief_across().wait_send()
    for k in range(2):
        fin_all(k).wait_send()
    kz_far(me).wait_send()
    if inner_n > 1:
        kz_near_all(0).wait_send()
        kz_near_all(2).wait_send()
    for g in range(1, groups):

        @pl.when(grp < g)
        def _():
            kx_copy(g, grp).wait_send()

    if n_pool > 1:
        page_all().wait()

    if n_pool > 1:
        last_all().wait()
    for store in stores:
        store.wait()


def store(*refs):
    count = (len(refs) - 2) // 3
    sem_in, sem_out = refs[-2:]
    through = refs[2 * count : 3 * count]
    rows = refs[0].shape[1] // 4
    pieces = [(0, (0, pl.ds(i * rows, rows))) for i in range(4)]
    pieces += [(i, (slice(None),)) for i in range(1, count)]
    loads = [
        pltpu.make_async_copy(refs[i].at[at], through[i].at[at], sem_in.at[j])
        for j, (i, at) in enumerate(pieces)
    ]
    saves = [
        pltpu.make_async_copy(through[i].at[at], refs[count + i].at[at], sem_out.at[j])
        for j, (i, at) in enumerate(pieces)
    ]
    for load in loads:
        load.start()
    for load, save in zip(loads, saves):
        load.wait()
        save.start()
    for save in saves:
        save.wait()


def local(n, n_pool, *args):
    (x, z, b, c, ld, skip, gain, seg, q, k, v, owner) = args
    rows, chans = x.shape[1:]
    heads = ld.shape[1]
    q_heads = q.shape[2] // HEAD_DIM
    p_rows = HEAD_P // n
    n_rows = STATE // n
    side = math.isqrt(n)
    groups = n // side
    owners_n = n // 2
    grp_heads = heads // n_pool
    page_rows = rows // n_pool
    tiles = chans // 128
    hbm = pl.BlockSpec(memory_space=pltpu.HBM)
    pages = (n_pool, page_rows, HEAD_DIM)
    states = (n_pool, grp_heads, p_rows, STATE)
    part = (4, owners_n, n_rows, chans // 2)
    dma = pltpu.SemaphoreType.DMA
    out = pl.pallas_call(
        functools.partial(kernel, n, n_pool),
        out_shape=(
            jax.ShapeDtypeStruct(x.shape, BF16),
            jax.ShapeDtypeStruct(q.shape, BF16),
            jax.ShapeDtypeStruct(states, F32),
            jax.ShapeDtypeStruct((1,) + pages, BF16),
            jax.ShapeDtypeStruct((1,) + pages, BF16),
        ),
        in_specs=[hbm] * 12,
        out_specs=[hbm] * 5,
        scratch_shapes=[
            pltpu.VMEM((rows, chans), BF16),
            pltpu.VMEM((rows, q_heads * HEAD_DIM), BF16),
            pltpu.VMEM((rows, chans), BF16),
            pltpu.VMEM((rows, chans), BF16),
            pltpu.VMEM((rows, STATE), BF16),
            pltpu.VMEM((rows, STATE), BF16),
            pltpu.VMEM((heads, rows), F32),
            pltpu.VMEM((1, heads), F32),
            pltpu.VMEM((1, chans), F32),
            pltpu.VMEM((1, rows), jnp.int32),
            pltpu.VMEM(owner.shape, jnp.int32),
            pltpu.VMEM((q_heads * rows, 2 * HEAD_DIM), BF16),
            pltpu.VMEM((n * rows, 2 * HEAD_DIM), BF16),
            pltpu.VMEM(part, BF16),
            pltpu.VMEM(part, BF16),
            pltpu.VMEM((4, groups, n_rows, chans // 2), BF16),
            pltpu.VMEM((4, groups + 1, n_rows, chans // 2), BF16),
            pltpu.VMEM(part, BF16),
            pltpu.VMEM(part, BF16),
            pltpu.VMEM((2, owners_n, 8, 128), F32),
            pltpu.VMEM((16, chans), F32),
            pltpu.VMEM((q_heads * rows, side * rows), F32),
            pltpu.VMEM((q_heads * rows, 128), F32),
            pltpu.VMEM((q_heads * rows, 128), F32),
            pltpu.VMEM((q_heads * rows, HEAD_DIM), F32),
            pltpu.VMEM((rows, chans), F32),
            pltpu.VMEM((rows, chans), F32),
            pltpu.VMEM((rows, chans), F32),
            pltpu.VMEM((n_pool, 2, page_rows, HEAD_DIM), BF16),
            pltpu.VMEM((128, tiles // 2 * n_rows), F32),
            pltpu.VMEM((2, owners_n, 2 * p_rows, tiles * n_rows), F32),
            pltpu.VMEM((2, owners_n, 2 * p_rows, tiles * n_rows), F32),
            pltpu.VMEM(states, F32),
            dma((11 + q_heads,)),
            dma((8,)),
            dma((2, 2)),
            dma((2, 4)),
            dma((2, 4)),
            dma((2, 4)),
            dma((2, 2)),
            dma((2, 3)),
            dma((2, 4)),
            dma((2, 2)),
        ],
        compiler_params=pltpu.CompilerParams(
            collective_id=0, has_side_effects=True, vmem_limit_bytes=60 * 1024 * 1024
        ),
    )(x, z, b, c, ld, skip.reshape(1, -1), gain.reshape(1, -1), seg, q, k, v, owner)
    out = pl.pallas_call(
        store,
        out_shape=tuple(jax.ShapeDtypeStruct(o.shape, o.dtype) for o in out),
        in_specs=[hbm] * 5,
        out_specs=[hbm] * 5,
        scratch_shapes=[pltpu.VMEM(o.shape, o.dtype) for o in out] + [dma((8,)), dma((8,))],
        compiler_params=pltpu.CompilerParams(vmem_limit_bytes=60 * 1024 * 1024),
    )(*out)
    mixer, attended, owned, keys, values = out
    return mixer, attended, owned[None], keys, values


def solution(mesh):
    return jax.shard_map(
        functools.partial(local, mesh.shape["seq"], mesh.shape["pool"]),
        mesh=mesh,
        in_specs=(
            P("pool", "seq", "head"),
            P("pool", "seq", "head"),
            P("pool", "seq", "head"),
            P("pool", "seq", "head"),
            P("pool", "head", "seq"),
            P("head"),
            P("head"),
            P("pool", "seq"),
            P("pool", "seq", "head"),
            P("pool", "seq", "head"),
            P("pool", "seq", "head"),
            P("pool", "head"),
        ),
        out_specs=(
            P("pool", "seq", "head"),
            P("pool", "seq", "head"),
            P("pool", None, "head", "seq", None),
            P("pool", None, "seq", "head"),
            P("pool", None, "seq", "head"),
        ),
        check_vma=False,
    )
```
